32 devices in a mesh: row: 4 (over y, x), col: 8 (over z, core).
Axes of the slice: x: 2, y: 2, z: 4, core: 2. Of those that a mesh axis runs over, the one named last changes fastest.
Arguments:
- qkv: bfloat16 [1536, 3, 4096], P('row', None, 'col'), may hold values from -22 to 22
- out_weight: bfloat16 [4096, 8192], P(None, 'col'), may hold values from -0.09375 to 0.09375
- cotangent: bfloat16 [1536, 8192], P('row', 'col'), may hold values from -6 to 6
- scene_lengths: int32 [32], P('row'), may hold values from 8 to 328, as said below
- bucket_ids: int32 [32], P('row'), may hold values from 0 to 7
- sensor_ids: int32 [32], P('row'), may hold values from 0 to 7
- gsd_ids: int32 [32], P('row'), may hold values from 0 to 15
- step_ids: int32 [32], P('row'), may hold values from 0 to 999
- step_table: bfloat16 [1000, 8192], P(None, 'col'), may hold values from -3 to 3
- gsd_table: bfloat16 [16, 8192], P(None, 'col'), may hold values from -3 to 3
- sensor_table: bfloat16 [8, 8192], P(None, 'col'), may hold values from -3 to 3
- bucket_table: bfloat16 [8, 8192], P(None, 'col'), may hold values from -3 to 3
Outputs:
- mixed: bfloat16 [1536, 8192], P('row', 'col')
- grad_qkv: bfloat16 [1536, 3, 4096], P('row', None, 'col')
- grad_weight: bfloat16 [4096, 8192], P(None, 'col')
The draws below stay inside these ranges and needn't reach their ends.
Inputs may be any that keep to these rules, and one draw needn't show every extreme that they name: `scene_lengths`: each block of 384 tokens holds 8 scenes whose lengths are positive multiples of 8 and sum to 384.
All inputs are finite; a program needn't handle non-finite values.
Results may differ from the reference program's by a relative error of at most 0.03.
Values may be sent and summed in bfloat16 or wider, within the bound.
A program may use at most 128 MiB of HBM per device.

```python
import jax
import jax.numpy as jnp
from jax import lax

D = 8192
HEADS = 32
HEAD = 128
TOK_ROW = 384
SCENES_ROW = 8
NT = 1000
NG = 16
NS = 8
NB = 8
HW = 4096
TOKENS = 1536
SCENES = 32
N_ROW = 4


def draw_qkv(key, part):
    base = jnp.clip(jax.random.normal(key, (TOKENS, 3, HW), jnp.float32), -4.0, 4.0)
    return base.astype(jnp.bfloat16)


def draw_scene_lengths(key, part):
    rows = SCENES // SCENES_ROW
    units = TOK_ROW // 8

    def one_row(row_key):
        cuts = jax.random.permutation(row_key, units - 1)[:SCENES_ROW - 1] + 1
        cuts = jnp.sort(cuts).astype(jnp.int32)
        edges = jnp.concatenate([jnp.zeros((1,), jnp.int32), cuts, jnp.full((1,), units, jnp.int32)])
        return (edges[1:] - edges[:-1]) * 8
    drawn = jax.vmap(one_row)(jax.random.split(key, rows))
    chosen_row = jax.random.randint(jax.random.fold_in(key, 101), (), 0, rows)
    chosen_place = jax.random.randint(jax.random.fold_in(key, 202), (), 0, SCENES_ROW)
    longest = TOK_ROW - 8 * (SCENES_ROW - 1)
    forced = jnp.where(jnp.arange(SCENES_ROW) == chosen_place, longest, 8).astype(jnp.int32)
    pick_row = (jnp.arange(rows) == chosen_row)[:, None]
    lengths = jnp.where(pick_row, forced[None, :], drawn)
    return lengths.reshape(-1).astype(jnp.int32)


def set_ends(values, key, low, high):
    shape = values.shape
    index_at = [jax.random.randint(jax.random.fold_in(key, axis), (), 0, shape[axis]) for axis in range(len(shape))]
    values = values.at[tuple(index_at)].set(low)
    longest = shape.index(max(shape))
    index_at[longest] = (index_at[longest] + 1) % shape[longest]
    return values.at[tuple(index_at)].set(high)


def shard_levels(rng, dims, cuts, low, high):
    def one(position, blocks):
        steps = jax.random.uniform(jax.random.fold_in(jax.random.fold_in(rng, 6), position), (blocks,), jnp.float32, low / len(cuts), high / len(cuts))
        return jnp.repeat(jnp.exp(steps), dims[position] // blocks).reshape((-1,) + (1,) * (len(dims) - position - 1))

    loudness = one(*cuts[0])
    for cut in cuts[1:]:
        loudness = loudness * one(*cut)
    return loudness


def normal_values(own_key, extent, deviation, limit, shards=(), kind=jnp.bfloat16):
    gain = shard_levels(own_key, extent, shards, -0.22, 0.18) if shards else 1.0
    values = jax.random.normal(own_key, extent, jnp.float32) * deviation * gain
    return jnp.minimum(jnp.maximum(values, -limit), limit).astype(kind)


def setup_inputs(seed: int = 0) -> dict:
    seeds = jax.random.split(jax.random.key(seed), 13)
    return {
        "qkv": draw_qkv(jax.random.fold_in(seeds[12], 71), 0),
        "out_weight": normal_values(seeds[1], (HW, D), HW ** -0.5, 0.09375, ((1, 8),)),
        "cotangent": normal_values(seeds[2], (TOKENS, D), 1.0, 6.0, ((0, 4), (1, 8))),
        "scene_lengths": draw_scene_lengths(jax.random.fold_in(seeds[12], 71), 0),
        "bucket_ids": set_ends(jax.random.randint(seeds[4], (SCENES,), 0, NB), jax.random.fold_in(seeds[4], 1), 0, NB - 1).astype(jnp.int32),
        "sensor_ids": set_ends(jax.random.randint(seeds[5], (SCENES,), 0, NS), jax.random.fold_in(seeds[5], 1), 0, NS - 1).astype(jnp.int32),
        "gsd_ids": set_ends(jax.random.randint(seeds[6], (SCENES,), 0, NG), jax.random.fold_in(seeds[6], 1), 0, NG - 1).astype(jnp.int32),
        "step_ids": set_ends(jax.random.randint(seeds[7], (SCENES,), 0, NT), jax.random.fold_in(seeds[7], 1), 0, NT - 1).astype(jnp.int32),
        "step_table": normal_values(seeds[8], (NT, D), 0.5, 3.0, ((1, 8),)),
        "gsd_table": normal_values(seeds[9], (NG, D), 0.5, 3.0, ((1, 8),)),
        "sensor_table": normal_values(seeds[10], (NS, D), 0.5, 3.0, ((1, 8),)),
        "bucket_table": normal_values(seeds[11], (NB, D), 0.5, 3.0, ((1, 8),)),
    }


def scene_of(lengths, count):
    ends = jnp.cumsum(lengths)
    places = jnp.arange(count)
    return jnp.sum((places[:, None] >= ends[None, :]).astype(jnp.int32), axis=1)


def lookup(ids, table):
    picks = (ids[:, None] == jnp.arange(table.shape[0])[None, :]).astype(table.dtype)
    return jnp.dot(picks, table, preferred_element_type=jnp.float32)


def attend(queries, keys, values, same):
    factor = HEAD ** -0.5
    scores = jnp.einsum("the,she->hts", queries.astype(jnp.float32), keys.astype(jnp.float32)) * factor
    scores = jnp.where(same[None], scores, -1e30)
    top = jnp.max(scores, axis=-1, keepdims=True)
    weights = jnp.exp(scores - top)
    probs = weights / jnp.sum(weights, axis=-1, keepdims=True)
    rounded = probs.astype(jnp.bfloat16)
    output = jnp.einsum("hts,she->the", rounded.astype(jnp.float32), values.astype(jnp.float32)).astype(jnp.bfloat16)
    return probs, rounded, output


def attend_back(queries, keys, values, probs, rounded, upstream):
    factor = HEAD ** -0.5
    upper = upstream.astype(jnp.float32)
    grad_values = jnp.einsum("hts,the->she", rounded.astype(jnp.float32), upper).astype(jnp.bfloat16)
    grad_probs = jnp.einsum("the,she->hts", upper, values.astype(jnp.float32))
    inner = jnp.sum(probs * grad_probs, axis=-1, keepdims=True)
    grad_scores = (probs * (grad_probs - inner)).astype(jnp.bfloat16).astype(jnp.float32)
    grad_queries = (jnp.einsum("hts,she->the", grad_scores, keys.astype(jnp.float32)) * factor).astype(jnp.bfloat16)
    grad_keys = (jnp.einsum("hts,the->she", grad_scores, queries.astype(jnp.float32)) * factor).astype(jnp.bfloat16)
    stacked = jnp.stack([grad_queries, grad_keys, grad_values], axis=1)
    return stacked.reshape(stacked.shape[0], 3, stacked.shape[2] * stacked.shape[3])


def reference(qkv, out_weight, cotangent, scene_lengths, bucket_ids, sensor_ids, gsd_ids, step_ids, step_table, gsd_table, sensor_table, bucket_table):
    gate_scene = lookup(step_ids, step_table) + lookup(gsd_ids, gsd_table)
    gate_scene = gate_scene + lookup(sensor_ids, sensor_table) + lookup(bucket_ids, bucket_table)
    lengths_rows = scene_lengths.reshape(N_ROW, SCENES_ROW)
    segments = jax.vmap(lambda lengths: scene_of(lengths, TOK_ROW))(lengths_rows)
    global_scene = segments + SCENES_ROW * jnp.arange(N_ROW, dtype=jnp.int32)[:, None]
    gate = gate_scene[global_scene.reshape(-1)]
    blocks = qkv.reshape(N_ROW, TOK_ROW, 3, HEADS, HEAD)

    def forward_row(items):
        block, segs = items
        same = segs[:, None] == segs[None, :]
        probs, rounded, output = attend(block[:, 0], block[:, 1], block[:, 2], same)
        return output.reshape(TOK_ROW, HW)

    attended = lax.map(forward_row, (blocks, segments)).reshape(TOKENS, HW)
    projected = jnp.dot(attended, out_weight, preferred_element_type=jnp.float32)
    mixed = (gate * projected).astype(jnp.bfloat16)
    gated = (gate * cotangent.astype(jnp.float32)).astype(jnp.bfloat16)
    upstream = jnp.dot(gated, out_weight.T, preferred_element_type=jnp.float32).astype(jnp.bfloat16)
    upstream_rows = upstream.reshape(N_ROW, TOK_ROW, HEADS, HEAD)

    def backward_row(items):
        block, segs, upper = items
        same = segs[:, None] == segs[None, :]
        probs, rounded, output = attend(block[:, 0], block[:, 1], block[:, 2], same)
        return attend_back(block[:, 0], block[:, 1], block[:, 2], probs, rounded, upper)

    grad_qkv = lax.map(backward_row, (blocks, segments, upstream_rows)).reshape(TOKENS, 3, HW)

    def add_row(total, items):
        attended_row, gated_row = items
        partial_sum = jnp.dot(attended_row.T, gated_row, preferred_element_type=jnp.float32).astype(jnp.bfloat16)
        partial_sum = lax.optimization_barrier(partial_sum)
        return total + partial_sum.astype(jnp.float32), None

    total, unused = lax.scan(add_row, jnp.zeros((HW, D), jnp.float32), (attended.reshape(N_ROW, TOK_ROW, HW), gated.reshape(N_ROW, TOK_ROW, D)))
    return mixed, grad_qkv, total.astype(jnp.bfloat16)
```

```python
import jax
import jax.numpy as jnp
from jax import lax
from jax.sharding import PartitionSpec as P

HEAD = 128


def scene_of(lengths, count):
    ends = jnp.cumsum(lengths)
    places = jnp.arange(count)
    return jnp.sum((places[:, None] >= ends[None, :]).astype(jnp.int32), axis=1)


def lookup(ids, table):
    picks = (ids[:, None] == jnp.arange(table.shape[0])[None, :]).astype(table.dtype)
    return jnp.dot(picks, table, preferred_element_type=jnp.float32)


def attend(queries, keys, values, same):
    factor = HEAD ** (-0.5)
    scores = jnp.einsum("the,she->hts", queries, keys, preferred_element_type=jnp.float32) * factor
    scores = jnp.where(same[None], scores, -1e30)
    top = jnp.max(scores, axis=-1, keepdims=True)
    weights = jnp.exp(scores - top)
    probs = weights / jnp.sum(weights, axis=-1, keepdims=True)
    rounded = probs.astype(jnp.bfloat16)
    output = jnp.einsum("hts,she->the", rounded, values, preferred_element_type=jnp.float32).astype(
        jnp.bfloat16
    )
    return (probs, rounded, output)


def attend_back(queries, keys, values, probs, rounded, upstream):
    factor = HEAD ** (-0.5)
    grad_values = jnp.einsum(
        "hts,the->she", rounded, upstream, preferred_element_type=jnp.float32
    ).astype(jnp.bfloat16)
    grad_probs = jnp.einsum("the,she->hts", upstream, values, preferred_element_type=jnp.float32)
    inner = jnp.sum(probs * grad_probs, axis=-1, keepdims=True)
    grad_scores = (probs * (grad_probs - inner)).astype(jnp.bfloat16)
    grad_queries = (
        jnp.einsum("hts,she->the", grad_scores, keys, preferred_element_type=jnp.float32) * factor
    ).astype(jnp.bfloat16)
    grad_keys = (
        jnp.einsum("hts,the->she", grad_scores, queries, preferred_element_type=jnp.float32)
        * factor
    ).astype(jnp.bfloat16)
    stacked = jnp.stack([grad_queries, grad_keys, grad_values], axis=1)
    return stacked.reshape(stacked.shape[0], 3, stacked.shape[2] * stacked.shape[3])


def on_device(
    qkv,
    out_weight,
    cotangent,
    scene_lengths,
    bucket_ids,
    sensor_ids,
    gsd_ids,
    step_ids,
    step_table,
    gsd_table,
    sensor_table,
    bucket_table,
):
    tok_rows = qkv.shape[0]
    local_width = qkv.shape[2]
    heads_here = local_width // HEAD
    gate_scene = lookup(step_ids, step_table) + lookup(gsd_ids, gsd_table)
    gate_scene = gate_scene + lookup(sensor_ids, sensor_table) + lookup(bucket_ids, bucket_table)
    segments = scene_of(scene_lengths, tok_rows)
    member = (segments[:, None] == jnp.arange(scene_lengths.shape[0])[None, :]).astype(jnp.float32)
    gate = jnp.dot(
        member, gate_scene, precision=lax.Precision.HIGHEST, preferred_element_type=jnp.float32
    )
    same = segments[:, None] == segments[None, :]
    block = qkv.reshape(tok_rows, 3, heads_here, HEAD)
    queries = block[:, 0]
    keys = block[:, 1]
    values = block[:, 2]
    probs, rounded, attended = attend(queries, keys, values, same)
    attended = attended.reshape(tok_rows, local_width)
    rows = out_weight
    whole = lax.all_gather(attended, "col", axis=1, tiled=True)
    projected = jnp.dot(
        whole,
        rows,
        preferred_element_type=jnp.float32,
    )
    mixed = (gate * projected).astype(jnp.bfloat16)
    gated = (gate * cotangent.astype(jnp.float32)).astype(jnp.bfloat16)
    rows = out_weight
    summed = lax.psum_scatter(
        lax.dot_general(
            rows, gated, (((1,), (1,)), ((), ())), preferred_element_type=jnp.float32
        ).astype(jnp.bfloat16),
        "col",
        scatter_dimension=0,
        tiled=True,
    )
    upstream = summed.T.reshape(tok_rows, heads_here, HEAD)
    grad_qkv = attend_back(queries, keys, values, probs, rounded, upstream)
    if lax.axis_size("row") > 4:
        partial_sum = lax.dot_general(
            whole, gated, (((0,), (0,)), ((), ())), preferred_element_type=jnp.float32
        )
        return (mixed, grad_qkv, lax.psum(partial_sum.astype(jnp.bfloat16), "row"))
    total = lax.dot_general(
        lax.all_gather(whole, "row", axis=0, tiled=True),
        lax.all_gather(gated, "row", axis=0, tiled=True),
        (((0,), (0,)), ((), ())),
        preferred_element_type=jnp.float32,
    ).astype(jnp.bfloat16)
    return (mixed, grad_qkv, total)


def solution(mesh):
    return jax.shard_map(
        on_device,
        mesh=mesh,
        in_specs=(
            P("row", None, "col"),
            P(None, "col"),
            P("row", "col"),
            P("row"),
            P("row"),
            P("row"),
            P("row"),
            P("row"),
            P(None, "col"),
            P(None, "col"),
            P(None, "col"),
            P(None, "col"),
        ),
        out_specs=(P("row", "col"), P("row", None, "col"), P(None, "col")),
        check_vma=False,
    )
```

```python
import jax
import jax.numpy as jnp
from jax import lax
from jax.experimental import pallas as pl
from jax.experimental.pallas import tpu as pltpu
from jax.sharding import PartitionSpec as P

HEAD = 128


def scene_of(lengths, count):
    ends = jnp.cumsum(lengths)
    places = jnp.arange(count)
    return jnp.sum((places[:, None] >= ends[None, :]).astype(jnp.int32), axis=1)


def lookup(ids, table):
    picks = (ids[:, None] == jnp.arange(table.shape[0])[None, :]).astype(table.dtype)
    return jnp.dot(picks, table, preferred_element_type=jnp.float32)


def attend(queries, keys, values, same):
    factor = HEAD ** (-0.5)
    scores = jnp.einsum("the,she->hts", queries, keys, preferred_element_type=jnp.float32) * factor
    scores = jnp.where(same[None], scores, -1e30)
    top = jnp.max(scores, axis=-1, keepdims=True)
    weights = jnp.exp(scores - top)
    probs = weights / jnp.sum(weights, axis=-1, keepdims=True)
    rounded = probs.astype(jnp.bfloat16)
    output = jnp.einsum("hts,she->the", rounded, values, preferred_element_type=jnp.float32).astype(
        jnp.bfloat16
    )
    return (probs, rounded, output)


def attend_back(queries, keys, values, probs, rounded, upstream):
    factor = HEAD ** (-0.5)
    grad_values = jnp.einsum(
        "hts,the->she", rounded, upstream, preferred_element_type=jnp.float32
    ).astype(jnp.bfloat16)
    grad_probs = jnp.einsum("the,she->hts", upstream, values, preferred_element_type=jnp.float32)
    inner = jnp.sum(probs * grad_probs, axis=-1, keepdims=True)
    grad_scores = (probs * (grad_probs - inner)).astype(jnp.bfloat16)
    grad_queries = (
        jnp.einsum("hts,she->the", grad_scores, keys, preferred_element_type=jnp.float32) * factor
    ).astype(jnp.bfloat16)
    grad_keys = (
        jnp.einsum("hts,the->she", grad_scores, queries, preferred_element_type=jnp.float32)
        * factor
    ).astype(jnp.bfloat16)
    stacked = jnp.stack([grad_queries, grad_keys, grad_values], axis=1)
    return stacked.reshape(stacked.shape[0], 3, stacked.shape[2] * stacked.shape[3])


def on_device(
    qkv,
    out_weight,
    cotangent,
    scene_lengths,
    bucket_ids,
    sensor_ids,
    gsd_ids,
    step_ids,
    step_table,
    gsd_table,
    sensor_table,
    bucket_table,
):
    tok_rows = qkv.shape[0]
    local_width = qkv.shape[2]
    heads_here = local_width // HEAD
    gate_scene = lookup(step_ids, step_table) + lookup(gsd_ids, gsd_table)
    gate_scene = gate_scene + lookup(sensor_ids, sensor_table) + lookup(bucket_ids, bucket_table)
    segments = scene_of(scene_lengths, tok_rows)
    member = (segments[:, None] == jnp.arange(scene_lengths.shape[0])[None, :]).astype(jnp.float32)
    gate = jnp.dot(
        member, gate_scene, precision=lax.Precision.HIGHEST, preferred_element_type=jnp.float32
    )
    same = segments[:, None] == segments[None, :]
    block = qkv.reshape(tok_rows, 3, heads_here, HEAD)
    queries = block[:, 0]
    keys = block[:, 1]
    values = block[:, 2]
    probs, rounded, attended = attend(queries, keys, values, same)
    attended = attended.reshape(tok_rows, local_width)
    rows = out_weight
    projected = jnp.dot(
        lax.all_gather(attended, "col", axis=1, tiled=True),
        rows,
        preferred_element_type=jnp.float32,
    )
    mixed = (gate * projected).astype(jnp.bfloat16)
    gated = (gate * cotangent.astype(jnp.float32)).astype(jnp.bfloat16)
    rows = out_weight
    summed = lax.psum_scatter(
        lax.dot_general(
            rows, gated, (((1,), (1,)), ((), ())), preferred_element_type=jnp.float32
        ).astype(jnp.bfloat16),
        "col",
        scatter_dimension=0,
        tiled=True,
    )
    upstream = summed.T.reshape(tok_rows, heads_here, HEAD)
    grad_qkv = attend_back(queries, keys, values, probs, rounded, upstream)
    partial_sum = lax.dot_general(
        lax.all_gather(attended, "col", axis=1, tiled=True),
        gated,
        (((0,), (0,)), ((), ())),
        preferred_element_type=jnp.float32,
    )
    total = lax.psum(partial_sum.astype(jnp.bfloat16), "row")
    return (mixed, grad_qkv, total)


def dot(a, b, dims):
    return lax.dot_general(a, b, (dims, ((), ())), preferred_element_type=jnp.float32)


def remote(src, dst, send, recv, device):
    return pltpu.make_async_remote_copy(
        src_ref=src,
        dst_ref=dst,
        send_sem=send,
        recv_sem=recv,
        device_id=device,
        device_id_type=pl.DeviceIdType.MESH,
    )


def fused_kernel(
    lengths,
    qkv,
    weight_hbm,
    cotangent,
    gate_scene,
    mixed_out,
    grad_out,
    total_hbm,
    weight,
    att,
    gat,
    gate,
    total_acc,
    probs_s,
    own,
    pair_send,
    pair_recv,
    line_send,
    line_recv,
    upstream,
    w_sem,
    out_sem,
    att_recv,
    gat_recv,
    pr_recv,
    lr_recv,
    z_sent,
    x_sent,
    y_sent,
    fx_sent,
    fy_sent,
    p_sent,
    g_sent,
    ps_sent,
    ls_sent,
):
    tok, width = cotangent.shape
    local = qkv.shape[2]
    heads = local // HEAD
    half = tok // 2
    nb = weight.shape[0]
    nz = nb // 2
    scenes = gate_scene.shape[0]
    factor = HEAD ** (-0.5)
    r = lax.axis_index("row")
    col = lax.axis_index("col")
    z = col // 2
    k = lax.rem(col, 2)
    xn = r + 1 - 2 * lax.rem(r, 2)
    yn = lax.rem(r + 2, 4)
    dn = 3 - r
    pair = {"col": col + 1 - 2 * k}
    to_x = {"row": xn}
    to_y = {"row": yn}

    barrier = pltpu.get_barrier_semaphore()
    peers = [pair, to_x, to_y] + [{"col": 2 * lax.rem(z + d, nz) + k} for d in range(1, nz)]
    for peer in peers:
        pl.semaphore_signal(
            barrier, inc=1, device_id=peer, device_id_type=pl.DeviceIdType.MESH
        )
    pl.semaphore_wait(barrier, len(peers))

    def load(b):
        return pltpu.make_async_copy(
            weight_hbm.at[pl.ds(b * local, local)], weight.at[b], w_sem.at[b]
        )

    for b in range(nb):
        load(b).start()

    def token_rows(row, part=None):
        if part is None:
            return pl.ds(pl.multiple_of(row * tok, tok), tok)
        return pl.ds(pl.multiple_of(row * tok + part * half, half), half)

    place_col = lax.broadcasted_iota(jnp.int32, (tok, 1), 0)
    place_row = lax.broadcasted_iota(jnp.int32, (1, tok), 1)
    seg_col = jnp.zeros((tok, 1), jnp.int32)
    seg_row = jnp.zeros((1, tok), jnp.int32)
    end = 0
    for s in range(scenes):
        end = end + lengths[s]
        seg_col = seg_col + (place_col >= end).astype(jnp.int32)
        seg_row = seg_row + (place_row >= end).astype(jnp.int32)
    value = jnp.broadcast_to(gate_scene[0:1, :], (tok, width))
    for s in range(1, scenes):
        value = jnp.where(seg_col == s, gate_scene[s : s + 1, :], value)
    gate[...] = value
    gat[token_rows(r), :] = (value * cotangent[...].astype(jnp.float32)).astype(jnp.bfloat16)

    def gat_copy(row, part, send, device):
        rows = gat.at[token_rows(row, part)]
        return remote(rows, rows, g_sent.at[send], gat_recv.at[row, 0 if part is None else part], device)

    gat_copy(r, None, 0, to_x).start()
    gat_copy(r, None, 1, to_y).start()

    same = seg_col == seg_row
    mine = 2 * z + k
    for h in range(heads):
        lanes = slice(h * HEAD, (h + 1) * HEAD)
        scores = dot(qkv[0, :, lanes], qkv[1, :, lanes], ((1,), (1,))) * factor
        scores = jnp.where(same, scores, -1e30)
        top = jnp.max(scores, axis=-1, keepdims=True)
        weights = jnp.exp(scores - top)
        probs = weights / jnp.sum(weights, axis=-1, keepdims=True)
        probs_s[h] = probs
        out = dot(probs.astype(jnp.bfloat16), qkv[2, :, lanes], ((1,), (0,)))
        att[mine, token_rows(r), lanes] = out.astype(jnp.bfloat16)

    orders = [sorted(range(nz), key=lambda o: (abs(o - p), o)) for p in range(nz)]

    def origin(j):
        picked = orders[0][j]
        for p in range(1, nz):
            picked = jnp.where(z == p, orders[p][j], picked)
        return picked

    origins = [origin(j) for j in range(nz)]

    def block(row, b, part=None):
        return att.at[b, token_rows(row, part)]

    def att_copy(row, b, part, send, device):
        ref = block(row, b, part)
        return remote(ref, ref, send, att_recv.at[row, b, 0 if part is None else part], device)

    def pass_on(row, o):
        return att_copy(row, 2 * o + k, None, p_sent.at[row, o], pair)

    def got(row, b, part=None):
        att_copy(row, b, part, p_sent.at[0, 0], pair).wait_recv()

    def upward(o):
        return att_copy(r, 2 * o + k, None, z_sent.at[o, 0], {"col": lax.rem(col + 2, 2 * nz)})

    def downward(o):
        return att_copy(
            r, 2 * o + k, None, z_sent.at[o, 1], {"col": lax.rem(col + 2 * nz - 2, 2 * nz)}
        )

    def stage_a(j):
        o = origins[j]
        if j > 0:
            got(r, 2 * o + k)

        @pl.when((o <= z) & (z < nz - 1))
        def _():
            upward(o).start()

        @pl.when((o >= z) & (z > 0))
        def _():
            downward(o).start()

        att_copy(r, 2 * o + k, None, x_sent.at[j], to_x).start()
        att_copy(r, 2 * o + k, None, y_sent.at[j], to_y).start()
        pass_on(r, o).start()

    def stage_b(j):
        o = origins[j]
        b = 2 * o + k
        got(xn, b)
        att_copy(xn, b, 0, fy_sent.at[j], to_y).start()
        pass_on(xn, o).start()
        got(yn, b)
        att_copy(yn, b, 1, fx_sent.at[j], to_x).start()
        pass_on(yn, o).start()

    def stage_c(j):
        o = origins[j]
        got(dn, 2 * o + k, 0)
        got(dn, 2 * o + k, 1)
        pass_on(dn, o).start()

    def stage_m(j):
        o = origins[j]
        got(r, 2 * o + 1 - k)

        def add(c, carry):
            b = 2 * o + c
            term = dot(att[b, token_rows(r), :], weight[b], ((1,), (0,)))
            if j == 0:
                total_acc[c] = term
            else:
                total_acc[c] += term
            return carry

        lax.fori_loop(0, 2, add, 0)

    def out_copy(b):
        return pltpu.make_async_copy(
            weight.at[b], total_hbm.at[pl.ds(pl.multiple_of(b * local, local), local)], out_sem.at[b]
        )

    def stage_w(j):
        o = origins[j]
        for row in (xn, yn, dn):
            got(row, 2 * o + 1 - k)

        def form(c, carry):
            b = 2 * o + c
            weight[b] = dot(att[b], gat[...], ((0,), (0,))).astype(jnp.bfloat16)
            out_copy(b).start()
            return carry

        lax.fori_loop(0, 2, form, 0)

    stage_a(0)

    for b in range(nb):
        load(b).wait()

    def pair_copy(t):
        return remote(pair_send.at[t], pair_recv.at[t], ps_sent.at[t], pr_recv.at[t], pair)

    def part_of(b):
        return dot(gat[token_rows(r), :], weight[b], ((1,), (1,)))

    def for_pair(i, carry):
        t = lax.rem(z + 1 + i, nz)
        pair_send[t] = part_of(2 * t + 1 - k).astype(jnp.bfloat16)
        pair_copy(t).start()
        return carry

    lax.fori_loop(0, nz, for_pair, 0)

    def for_self(i, carry):
        t = lax.rem(z + 1 + i, nz)
        own[t] = part_of(2 * t + k)
        return carry

    lax.fori_loop(0, nz, for_self, 0)

    def line_copy(t):
        return remote(
            line_send.at[t], line_recv.at[z], ls_sent.at[t], lr_recv.at[z], {"col": 2 * t + k}
        )

    for d in range(1, nz):
        t = lax.rem(z + d, nz)
        pair_copy(t).wait_recv()
        line_send[t] = (own[t] + pair_recv[t].astype(jnp.float32)).astype(jnp.bfloat16)
        line_copy(t).start()

    stage_a(1)
    gat_copy(xn, None, 0, to_x).wait_recv()
    gat_copy(xn, 0, 2, to_y).start()
    gat_copy(yn, None, 0, to_x).wait_recv()
    gat_copy(yn, 1, 3, to_x).start()
    stage_b(0)
    stage_a(2)
    stage_m(0)
    stage_c(0)
    stage_b(1)
    stage_a(3)
    stage_m(1)
    stage_c(1)

    pair_copy(z).wait_recv()
    summed = own[z] + pair_recv[z].astype(jnp.float32)
    for d in range(1, nz):
        t = lax.rem(z + d, nz)
        remote(
            line_send.at[t], line_recv.at[t], ls_sent.at[t], lr_recv.at[t], {"col": 2 * t + k}
        ).wait_recv()
        summed = summed + line_recv[t].astype(jnp.float32)
    upstream[...] = summed.astype(jnp.bfloat16)
    for h in range(heads):
        lanes = slice(h * HEAD, (h + 1) * HEAD)
        upper = upstream[:, lanes]
        probs = probs_s[h]
        grad_out[2, :, lanes] = dot(probs.astype(jnp.bfloat16), upper, ((0,), (0,))).astype(
            jnp.bfloat16
        )
        grad_probs = dot(upper, qkv[2, :, lanes], ((1,), (1,)))
        inner = jnp.sum(probs * grad_probs, axis=-1, keepdims=True)
        grad_scores = (probs * (grad_probs - inner)).astype(jnp.bfloat16)
        grad_out[0, :, lanes] = (
            dot(grad_scores, qkv[1, :, lanes], ((1,), (0,))) * factor
        ).astype(jnp.bfloat16)
        grad_out[1, :, lanes] = (
            dot(grad_scores, qkv[0, :, lanes], ((0,), (0,))) * factor
        ).astype(jnp.bfloat16)

    stage_b(2)
    stage_m(2)
    stage_m(3)
    mixed_out[...] = (gate[...] * (total_acc[0] + total_acc[1])).astype(jnp.bfloat16)
    gat_copy(dn, 0, 0, to_x).wait_recv()
    gat_copy(dn, 1, 0, to_x).wait_recv()
    stage_c(2)
    stage_w(0)
    stage_b(3)
    stage_w(1)
    stage_c(3)
    stage_w(2)
    stage_w(3)

    gat_copy(r, None, 0, to_x).wait_send()
    gat_copy(r, None, 1, to_y).wait_send()
    gat_copy(xn, 0, 2, to_y).wait_send()
    gat_copy(yn, 1, 3, to_x).wait_send()
    for j in range(nz):
        o = origins[j]
        b = 2 * o + k

        @pl.when((o <= z) & (z < nz - 1))
        def _():
            upward(o).wait_send()

        @pl.when((o >= z) & (z > 0))
        def _():
            downward(o).wait_send()

        att_copy(r, b, None, x_sent.at[j], to_x).wait_send()
        att_copy(r, b, None, y_sent.at[j], to_y).wait_send()
        att_copy(xn, b, 0, fy_sent.at[j], to_y).wait_send()
        att_copy(yn, b, 1, fx_sent.at[j], to_x).wait_send()
        for row in (r, xn, yn, dn):
            pass_on(row, o).wait_send()
        pair_copy(j).wait_send()
        out_copy(2 * j).wait()
        out_copy(2 * j + 1).wait()
    for d in range(1, nz):
        line_copy(lax.rem(z + d, nz)).wait_send()


def fused_device(
    qkv,
    out_weight,
    cotangent,
    scene_lengths,
    bucket_ids,
    sensor_ids,
    gsd_ids,
    step_ids,
    step_table,
    gsd_table,
    sensor_table,
    bucket_table,
):
    rows = lax.axis_size("row")
    cols = lax.axis_size("col")
    nz = cols // 2
    tok, width = cotangent.shape
    local = qkv.shape[2]
    gate_scene = lookup(step_ids, step_table) + lookup(gsd_ids, gsd_table)
    gate_scene = gate_scene + lookup(sensor_ids, sensor_table) + lookup(bucket_ids, bucket_table)
    dma = pltpu.SemaphoreType.DMA
    bf16 = jnp.bfloat16
    mixed, grad, total = pl.pallas_call(
        fused_kernel,
        out_shape=(
            jax.ShapeDtypeStruct((tok, width), bf16),
            jax.ShapeDtypeStruct((3, tok, local), bf16),
            jax.ShapeDtypeStruct(out_weight.shape, bf16),
        ),
        in_specs=[
            pl.BlockSpec(memory_space=pltpu.SMEM),
            pl.BlockSpec(memory_space=pltpu.VMEM),
            pl.BlockSpec(memory_space=pl.ANY),
            pl.BlockSpec(memory_space=pltpu.VMEM),
            pl.BlockSpec(memory_space=pltpu.VMEM),
        ],
        out_specs=(
            pl.BlockSpec(memory_space=pltpu.VMEM),
            pl.BlockSpec(memory_space=pltpu.VMEM),
            pl.BlockSpec(memory_space=pl.ANY),
        ),
        scratch_shapes=[
            pltpu.VMEM((cols, local, width), bf16),
            pltpu.VMEM((cols, rows * tok, local), bf16),
            pltpu.VMEM((rows * tok, width), bf16),
            pltpu.VMEM((tok, width), jnp.float32),
            pltpu.VMEM((2, tok, width), jnp.float32),
            pltpu.VMEM((local // HEAD, tok, tok), jnp.float32),
            pltpu.VMEM((nz, tok, local), jnp.float32),
            pltpu.VMEM((nz, tok, local), bf16),
            pltpu.VMEM((nz, tok, local), bf16),
            pltpu.VMEM((nz, tok, local), bf16),
            pltpu.VMEM((nz, tok, local), bf16),
            pltpu.VMEM((tok, local), bf16),
            dma((cols,)),
            dma((cols,)),
            dma((rows, cols, 2)),
            dma((rows, 2)),
            dma((nz,)),
            dma((nz,)),
            dma((nz, 2)),
            dma((nz,)),
            dma((nz,)),
            dma((nz,)),
            dma((nz,)),
            dma((rows, nz)),
            dma((4,)),
            dma((nz,)),
            dma((nz,)),
        ],
        compiler_params=pltpu.CompilerParams(
            collective_id=0, has_side_effects=True, vmem_limit_bytes=60 * 2**20
        ),
        cost_estimate=pl.CostEstimate(
            flops=2 * (rows + 2) * tok * out_weight.shape[0] * width,
            bytes_accessed=4 * out_weight.shape[0] * width,
            transcendentals=0,
        ),
    )(scene_lengths, jnp.transpose(qkv, (1, 0, 2)), out_weight, cotangent, gate_scene)
    return (mixed, jnp.transpose(grad, (1, 0, 2)), total)


def solution(mesh):
    planes = mesh.shape["row"] == 4 and mesh.shape["col"] == 8
    return jax.shard_map(
        fused_device if planes else on_device,
        mesh=mesh,
        in_specs=(
            P("row", None, "col"),
            P(None, "col"),
            P("row", "col"),
            P("row"),
            P("row"),
            P("row"),
            P("row"),
            P("row"),
            P(None, "col"),
            P(None, "col"),
            P(None, "col"),
            P(None, "col"),
        ),
        out_specs=(P("row", "col"), P("row", None, "col"), P(None, "col")),
        check_vma=False,
    )
```

```python
import jax
import jax.numpy as jnp
from jax import lax
from jax.experimental import pallas as pl
from jax.experimental.pallas import tpu as pltpu
from jax.sharding import PartitionSpec as P

HEAD = 128


def scene_of(lengths, count):
    ends = jnp.cumsum(lengths)
    places = jnp.arange(count)
    return jnp.sum((places[:, None] >= ends[None, :]).astype(jnp.int32), axis=1)


def lookup(ids, table):
    picks = (ids[:, None] == jnp.arange(table.shape[0])[None, :]).astype(table.dtype)
    return jnp.dot(picks, table, preferred_element_type=jnp.float32)


def attend(queries, keys, values, same):
    factor = HEAD ** (-0.5)
    scores = jnp.einsum("the,she->hts", queries, keys, preferred_element_type=jnp.float32) * factor
    scores = jnp.where(same[None], scores, -1e30)
    top = jnp.max(scores, axis=-1, keepdims=True)
    weights = jnp.exp(scores - top)
    probs = weights / jnp.sum(weights, axis=-1, keepdims=True)
    rounded = probs.astype(jnp.bfloat16)
    output = jnp.einsum("hts,she->the", rounded, values, preferred_element_type=jnp.float32).astype(
        jnp.bfloat16
    )
    return (probs, rounded, output)


def attend_back(queries, keys, values, probs, rounded, upstream):
    factor = HEAD ** (-0.5)
    grad_values = jnp.einsum(
        "hts,the->she", rounded, upstream, preferred_element_type=jnp.float32
    ).astype(jnp.bfloat16)
    grad_probs = jnp.einsum("the,she->hts", upstream, values, preferred_element_type=jnp.float32)
    inner = jnp.sum(probs * grad_probs, axis=-1, keepdims=True)
    grad_scores = (probs * (grad_probs - inner)).astype(jnp.bfloat16)
    grad_queries = (
        jnp.einsum("hts,she->the", grad_scores, keys, preferred_element_type=jnp.float32) * factor
    ).astype(jnp.bfloat16)
    grad_keys = (
        jnp.einsum("hts,the->she", grad_scores, queries, preferred_element_type=jnp.float32)
        * factor
    ).astype(jnp.bfloat16)
    stacked = jnp.stack([grad_queries, grad_keys, grad_values], axis=1)
    return stacked.reshape(stacked.shape[0], 3, stacked.shape[2] * stacked.shape[3])


def on_device(
    qkv,
    out_weight,
    cotangent,
    scene_lengths,
    bucket_ids,
    sensor_ids,
    gsd_ids,
    step_ids,
    step_table,
    gsd_table,
    sensor_table,
    bucket_table,
):
    tok_rows = qkv.shape[0]
    local_width = qkv.shape[2]
    heads_here = local_width // HEAD
    gate_scene = lookup(step_ids, step_table) + lookup(gsd_ids, gsd_table)
    gate_scene = gate_scene + lookup(sensor_ids, sensor_table) + lookup(bucket_ids, bucket_table)
    segments = scene_of(scene_lengths, tok_rows)
    member = (segments[:, None] == jnp.arange(scene_lengths.shape[0])[None, :]).astype(jnp.float32)
    gate = jnp.dot(
        member, gate_scene, precision=lax.Precision.HIGHEST, preferred_element_type=jnp.float32
    )
    same = segments[:, None] == segments[None, :]
    block = qkv.reshape(tok_rows, 3, heads_here, HEAD)
    queries = block[:, 0]
    keys = block[:, 1]
    values = block[:, 2]
    probs, rounded, attended = attend(queries, keys, values, same)
    attended = attended.reshape(tok_rows, local_width)
    rows = out_weight
    projected = jnp.dot(
        lax.all_gather(attended, "col", axis=1, tiled=True),
        rows,
        preferred_element_type=jnp.float32,
    )
    mixed = (gate * projected).astype(jnp.bfloat16)
    gated = (gate * cotangent.astype(jnp.float32)).astype(jnp.bfloat16)
    rows = out_weight
    summed = lax.psum_scatter(
        lax.dot_general(
            rows, gated, (((1,), (1,)), ((), ())), preferred_element_type=jnp.float32
        ).astype(jnp.bfloat16),
        "col",
        scatter_dimension=0,
        tiled=True,
    )
    upstream = summed.T.reshape(tok_rows, heads_here, HEAD)
    grad_qkv = attend_back(queries, keys, values, probs, rounded, upstream)
    partial_sum = lax.dot_general(
        lax.all_gather(attended, "col", axis=1, tiled=True),
        gated,
        (((0,), (0,)), ((), ())),
        preferred_element_type=jnp.float32,
    )
    total = lax.psum(partial_sum.astype(jnp.bfloat16), "row")
    return (mixed, grad_qkv, total)


def dot(a, b, dims):
    return lax.dot_general(a, b, (dims, ((), ())), preferred_element_type=jnp.float32)


def remote(src, dst, send, recv, device):
    return pltpu.make_async_remote_copy(
        src_ref=src,
        dst_ref=dst,
        send_sem=send,
        recv_sem=recv,
        device_id=device,
        device_id_type=pl.DeviceIdType.MESH,
    )


def origins_of(z, nz):
    orders = [sorted(range(nz), key=lambda o: (abs(o - p), o)) for p in range(nz)]
    origins = []
    for j in range(nz):
        picked = orders[0][j]
        for p in range(1, nz):
            picked = jnp.where(z == p, orders[p][j], picked)
        origins.append(picked)
    return origins


def last_kernel(
    mixed_in,
    grad_in,
    total_head,
    att_tail,
    gat_all,
    mixed_out,
    grad_out,
    total_out,
    mixed,
    grad,
    head,
    att,
    gat,
    tail,
    in_sem,
    head_sem,
    att_sem,
    out_sem,
    total_sem,
):
    early, parts, local, width = head.shape
    late = att.shape[0]
    origins = origins_of(lax.axis_index("col") // 2, early + late)

    def place(j, c):
        return total_out.at[pl.ds(pl.multiple_of((2 * origins[j] + c) * local, local), local)]

    gat_load = pltpu.make_async_copy(gat_all, gat, in_sem.at[0])
    gat_load.start()
    att_loads = {}
    for j in range(late):
        for c in range(parts):
            att_loads[j, c] = pltpu.make_async_copy(att_tail.at[j, c], att.at[j, c], att_sem.at[j, c])
            att_loads[j, c].start()
    moves = []
    for j in range(early):
        for c in range(parts):
            moves.append((
                pltpu.make_async_copy(total_head.at[j, c], head.at[j, c], head_sem.at[j, c]),
                pltpu.make_async_copy(head.at[j, c], place(j, c), total_sem.at[j, c]),
            ))
    moves.append((
        pltpu.make_async_copy(mixed_in, mixed, in_sem.at[1]),
        pltpu.make_async_copy(mixed, mixed_out, out_sem.at[0]),
    ))
    moves.append((
        pltpu.make_async_copy(grad_in, grad, in_sem.at[2]),
        pltpu.make_async_copy(grad, grad_out, out_sem.at[1]),
    ))
    for load, store in moves:
        load.start()
    gat_load.wait()
    steps = late * parts
    share = -(-len(moves) // steps)
    stores = []
    for i in range(steps):
        j, c = divmod(i, parts)
        att_loads[j, c].wait()
        tail[j, c] = dot(att[j, c], gat[...], ((0,), (0,))).astype(jnp.bfloat16)
        stores.append(pltpu.make_async_copy(tail.at[j, c], place(early + j, c), total_sem.at[early + j, c]))
        stores[-1].start()
        for load, store in moves[i * share : (i + 1) * share]:
            load.wait()
            store.start()
            stores.append(store)
    for store in stores:
        store.wait()


def fused_kernel(
    lengths,
    bucket_ids,
    sensor_ids,
    gsd_ids,
    step_ids,
    qkv,
    weight_hbm,
    cotangent,
    step_hbm,
    gsd_table,
    sensor_table,
    bucket_table,
    mixed_out,
    grad_out,
    total_head,
    att_tail,
    gat_all,
    step_table,
    weight,
    att,
    gat,
    gate,
    total_acc,
    probs_s,
    own,
    pair_send,
    pair_recv,
    line_send,
    line_recv,
    upstream,
    w_sem,
    step_sem,
    out_sem,
    tail_sem,
    gat_sem,
    att_recv,
    gat_recv,
    pr_recv,
    lr_recv,
    z_sent,
    x_sent,
    y_sent,
    fx_sent,
    fy_sent,
    p_sent,
    g_sent,
    ps_sent,
    ls_sent,
):
    tok, width = cotangent.shape
    local = qkv.shape[2]
    heads = local // HEAD
    half = tok // 2
    nb = weight.shape[0]
    nz = nb // 2
    scenes = lengths.shape[0]
    early = total_head.shape[0]
    factor = HEAD ** (-0.5)
    r = lax.axis_index("row")
    col = lax.axis_index("col")
    z = col // 2
    k = lax.rem(col, 2)
    xn = r + 1 - 2 * lax.rem(r, 2)
    yn = lax.rem(r + 2, 4)
    dn = 3 - r
    pair = {"col": col + 1 - 2 * k}
    to_x = {"row": xn}
    to_y = {"row": yn}

    barrier = pltpu.get_barrier_semaphore()
    peers = [pair, to_x, to_y] + [{"col": 2 * lax.rem(z + d, nz) + k} for d in range(1, nz)]
    for peer in peers:
        pl.semaphore_signal(
            barrier, inc=1, device_id=peer, device_id_type=pl.DeviceIdType.MESH
        )
    pl.semaphore_wait(barrier, len(peers))

    def load(b):
        return pltpu.make_async_copy(
            weight_hbm.at[pl.ds(b * local, local)], weight.at[b], w_sem.at[b]
        )

    step_load = pltpu.make_async_copy(step_hbm, step_table, step_sem)
    step_load.start()
    for b in range(nb):
        load(b).start()

    def token_rows(row, part=None):
        if part is None:
            return pl.ds(pl.multiple_of(row * tok, tok), tok)
        return pl.ds(pl.multiple_of(row * tok + part * half, half), half)

    place_col = lax.broadcasted_iota(jnp.int32, (tok, 1), 0)
    place_row = lax.broadcasted_iota(jnp.int32, (1, tok), 1)
    seg_col = jnp.zeros((tok, 1), jnp.int32)
    seg_row = jnp.zeros((1, tok), jnp.int32)
    end = 0
    for s in range(scenes):
        end = end + lengths[s]
        seg_col = seg_col + (place_col >= end).astype(jnp.int32)
        seg_row = seg_row + (place_row >= end).astype(jnp.int32)

    same = seg_col == seg_row
    mine = 2 * z + k
    for h in range(heads):
        lanes = slice(h * HEAD, (h + 1) * HEAD)
        scores = dot(qkv[0, :, lanes], qkv[1, :, lanes], ((1,), (1,))) * factor
        scores = jnp.where(same, scores, -1e30)
        top = jnp.max(scores, axis=-1, keepdims=True)
        weights = jnp.exp(scores - top)
        probs = weights / jnp.sum(weights, axis=-1, keepdims=True)
        probs_s[h] = probs
        out = dot(probs.astype(jnp.bfloat16), qkv[2, :, lanes], ((1,), (0,)))
        att[mine, token_rows(r), lanes] = out.astype(jnp.bfloat16)

    origins = origins_of(z, nz)

    def block(row, b, part=None):
        return att.at[b, token_rows(row, part)]

    def att_copy(row, b, part, send, device):
        ref = block(row, b, part)
        return remote(ref, ref, send, att_recv.at[row, b, 0 if part is None else part], device)

    def pass_on(row, o):
        return att_copy(row, 2 * o + k, None, p_sent.at[row, o], pair)

    def got(row, b, part=None):
        att_copy(row, b, part, p_sent.at[0, 0], pair).wait_recv()

    def upward(o):
        return att_copy(r, 2 * o + k, None, z_sent.at[o, 0], {"col": lax.rem(col + 2, 2 * nz)})

    def downward(o):
        return att_copy(
            r, 2 * o + k, None, z_sent.at[o, 1], {"col": lax.rem(col + 2 * nz - 2, 2 * nz)}
        )

    def stage_a(j):
        o = origins[j]
        if j > 0:
            got(r, 2 * o + k)

        @pl.when((o <= z) & (z < nz - 1))
        def _():
            upward(o).start()

        @pl.when((o >= z) & (z > 0))
        def _():
            downward(o).start()

        att_copy(r, 2 * o + k, None, x_sent.at[j], to_x).start()
        att_copy(r, 2 * o + k, None, y_sent.at[j], to_y).start()
        pass_on(r, o).start()

    def stage_b(j):
        o = origins[j]
        b = 2 * o + k
        got(xn, b)
        att_copy(xn, b, 0, fy_sent.at[j], to_y).start()
        pass_on(xn, o).start()
        got(yn, b)
        att_copy(yn, b, 1, fx_sent.at[j], to_x).start()
        pass_on(yn, o).start()

    def stage_c(j):
        o = origins[j]
        got(dn, 2 * o + k, 0)
        got(dn, 2 * o + k, 1)
        pass_on(dn, o).start()

    def stage_m(j):
        o = origins[j]
        got(r, 2 * o + 1 - k)

        def add(c, carry):
            b = 2 * o + c
            term = dot(att[b, token_rows(r), :], weight[b], ((1,), (0,)))
            if j == 0:
                total_acc[c] = term
            else:
                total_acc[c] += term
            return carry

        lax.fori_loop(0, 2, add, 0)

    def out_copy(j, c):
        return pltpu.make_async_copy(
            weight.at[2 * origins[j] + c], total_head.at[j, c], out_sem.at[j, c]
        )

    def tail_copy(j, c):
        return pltpu.make_async_copy(
            att.at[2 * origins[j] + c], att_tail.at[j - early, c], tail_sem.at[j - early, c]
        )

    gat_out = pltpu.make_async_copy(gat, gat_all, gat_sem)

    def stage_w(j):
        o = origins[j]
        for row in (xn, yn, dn):
            got(row, 2 * o + 1 - k)

        def form(c, carry):
            b = 2 * o + c
            weight[b] = dot(att[b], gat[...], ((0,), (0,))).astype(jnp.bfloat16)
            out_copy(j, c).start()
            return carry

        if j < early:
            lax.fori_loop(0, 2, form, 0)
        else:
            for c in range(2):
                tail_copy(j, c).start()

    stage_a(0)

    def picks(ids, table):
        count = table.shape[0]
        which = lax.broadcasted_iota(jnp.int32, (scenes, count), 0)
        place = lax.broadcasted_iota(jnp.int32, (scenes, count), 1)
        wanted = jnp.zeros((scenes, count), jnp.int32)
        for s in range(scenes):
            wanted = jnp.where(which == s, ids[s], wanted)
        chosen = jnp.where(place == wanted, 1.0, 0.0).astype(table.dtype)
        return dot(chosen, table[...], ((1,), (0,)))

    step_load.wait()
    gate_scene = picks(step_ids, step_table) + picks(gsd_ids, gsd_table)
    gate_scene = gate_scene + picks(sensor_ids, sensor_table) + picks(bucket_ids, bucket_table)
    value = jnp.broadcast_to(gate_scene[0:1, :], (tok, width))
    for s in range(1, scenes):
        value = jnp.where(seg_col == s, gate_scene[s : s + 1, :], value)
    gate[...] = value
    gat[token_rows(r), :] = (value * cotangent[...].astype(jnp.float32)).astype(jnp.bfloat16)

    def gat_copy(row, part, send, device):
        rows = gat.at[token_rows(row, part)]
        return remote(rows, rows, g_sent.at[send], gat_recv.at[row, 0 if part is None else part], device)

    gat_copy(r, None, 0, to_x).start()
    gat_copy(r, None, 1, to_y).start()

    for b in range(nb):
        load(b).wait()

    def pair_copy(t):
        return remote(pair_send.at[t], pair_recv.at[t], ps_sent.at[t], pr_recv.at[t], pair)

    def part_of(b):
        return dot(gat[token_rows(r), :], weight[b], ((1,), (1,)))

    def for_pair(i, carry):
        t = lax.rem(z + 1 + i, nz)
        pair_send[t] = part_of(2 * t + 1 - k).astype(jnp.bfloat16)
        pair_copy(t).start()
        return carry

    lax.fori_loop(0, nz, for_pair, 0)

    def for_self(i, carry):
        t = lax.rem(z + 1 + i, nz)
        own[t] = part_of(2 * t + k)
        return carry

    lax.fori_loop(0, nz, for_self, 0)

    def line_copy(t):
        return remote(
            line_send.at[t], line_recv.at[z], ls_sent.at[t], lr_recv.at[z], {"col": 2 * t + k}
        )

    for d in range(1, nz):
        t = lax.rem(z + d, nz)
        pair_copy(t).wait_recv()
        line_send[t] = (own[t] + pair_recv[t].astype(jnp.float32)).astype(jnp.bfloat16)
        line_copy(t).start()

    stage_b(0)
    stage_a(1)
    stage_m(0)
    stage_c(0)
    stage_a(2)
    gat_copy(xn, None, 0, to_x).wait_recv()
    gat_copy(xn, 0, 2, to_y).start()
    gat_copy(yn, None, 0, to_x).wait_recv()
    gat_copy(yn, 1, 3, to_x).start()
    stage_b(1)
    stage_a(3)
    stage_m(1)
    stage_c(1)
    gat_copy(dn, 0, 0, to_x).wait_recv()
    gat_copy(dn, 1, 0, to_x).wait_recv()
    gat_out.start()
    stage_w(0)

    pair_copy(z).wait_recv()
    summed = own[z] + pair_recv[z].astype(jnp.float32)
    for d in range(1, nz):
        t = lax.rem(z + d, nz)
        remote(
            line_send.at[t], line_recv.at[t], ls_sent.at[t], lr_recv.at[t], {"col": 2 * t + k}
        ).wait_recv()
        summed = summed + line_recv[t].astype(jnp.float32)
    upstream[...] = summed.astype(jnp.bfloat16)
    for h in range(heads):
        lanes = slice(h * HEAD, (h + 1) * HEAD)
        upper = upstream[:, lanes]
        probs = probs_s[h]
        grad_out[2, :, lanes] = dot(probs.astype(jnp.bfloat16), upper, ((0,), (0,))).astype(
            jnp.bfloat16
        )
        grad_probs = dot(upper, qkv[2, :, lanes], ((1,), (1,)))
        inner = jnp.sum(probs * grad_probs, axis=-1, keepdims=True)
        grad_scores = (probs * (grad_probs - inner)).astype(jnp.bfloat16)
        grad_out[0, :, lanes] = (
            dot(grad_scores, qkv[1, :, lanes], ((1,), (0,))) * factor
        ).astype(jnp.bfloat16)
        grad_out[1, :, lanes] = (
            dot(grad_scores, qkv[0, :, lanes], ((0,), (0,))) * factor
        ).astype(jnp.bfloat16)

    stage_b(2)
    stage_m(2)
    stage_m(3)
    mixed_out[...] = (gate[...] * (total_acc[0] + total_acc[1])).astype(jnp.bfloat16)
    stage_c(2)
    stage_w(1)
    stage_b(3)
    stage_w(2)
    stage_c(3)
    stage_w(3)

    gat_copy(r, None, 0, to_x).wait_send()
    gat_copy(r, None, 1, to_y).wait_send()
    gat_copy(xn, 0, 2, to_y).wait_send()
    gat_copy(yn, 1, 3, to_x).wait_send()
    for j in range(nz):
        o = origins[j]
        b = 2 * o + k

        @pl.when((o <= z) & (z < nz - 1))
        def _():
            upward(o).wait_send()

        @pl.when((o >= z) & (z > 0))
        def _():
            downward(o).wait_send()

        att_copy(r, b, None, x_sent.at[j], to_x).wait_send()
        att_copy(r, b, None, y_sent.at[j], to_y).wait_send()
        att_copy(xn, b, 0, fy_sent.at[j], to_y).wait_send()
        att_copy(yn, b, 1, fx_sent.at[j], to_x).wait_send()
        for row in (r, xn, yn, dn):
            pass_on(row, o).wait_send()
        pair_copy(j).wait_send()
        for c in range(2):
            (out_copy if j < early else tail_copy)(j, c).wait()
    for d in range(1, nz):
        line_copy(lax.rem(z + d, nz)).wait_send()
    gat_out.wait()


def fused_device(
    qkv,
    out_weight,
    cotangent,
    scene_lengths,
    bucket_ids,
    sensor_ids,
    gsd_ids,
    step_ids,
    step_table,
    gsd_table,
    sensor_table,
    bucket_table,
):
    rows = lax.axis_size("row")
    cols = lax.axis_size("col")
    nz = cols // 2
    tok, width = cotangent.shape
    local = qkv.shape[2]
    early = nz - 1
    late = nz - early
    dma = pltpu.SemaphoreType.DMA
    bf16 = jnp.bfloat16
    mixed, grad, head, tail, gat_all = pl.pallas_call(
        fused_kernel,
        out_shape=(
            jax.ShapeDtypeStruct((tok, width), bf16),
            jax.ShapeDtypeStruct((3, tok, local), bf16),
            jax.ShapeDtypeStruct((early, 2, local, width), bf16),
            jax.ShapeDtypeStruct((late, 2, rows * tok, local), bf16),
            jax.ShapeDtypeStruct((rows * tok, width), bf16),
        ),
        in_specs=[pl.BlockSpec(memory_space=pltpu.SMEM)] * 5
        + [
            pl.BlockSpec(memory_space=pltpu.VMEM),
            pl.BlockSpec(memory_space=pl.ANY),
            pl.BlockSpec(memory_space=pltpu.VMEM),
            pl.BlockSpec(memory_space=pl.ANY),
        ]
        + [pl.BlockSpec(memory_space=pltpu.VMEM)] * 3,
        out_specs=(pl.BlockSpec(memory_space=pltpu.VMEM),) * 2
        + (pl.BlockSpec(memory_space=pl.ANY),) * 3,
        scratch_shapes=[
            pltpu.VMEM(step_table.shape, bf16),
            pltpu.VMEM((cols, local, width), bf16),
            pltpu.VMEM((cols, rows * tok, local), bf16),
            pltpu.VMEM((rows * tok, width), bf16),
            pltpu.VMEM((tok, width), jnp.float32),
            pltpu.VMEM((2, tok, width), jnp.float32),
            pltpu.VMEM((local // HEAD, tok, tok), jnp.float32),
            pltpu.VMEM((nz, tok, local), jnp.float32),
            pltpu.VMEM((nz, tok, local), bf16),
            pltpu.VMEM((nz, tok, local), bf16),
            pltpu.VMEM((nz, tok, local), bf16),
            pltpu.VMEM((nz, tok, local), bf16),
            pltpu.VMEM((tok, local), bf16),
            dma((cols,)),
            dma,
            dma((early, 2)),
            dma((late, 2)),
            dma,
            dma((rows, cols, 2)),
            dma((rows, 2)),
            dma((nz,)),
            dma((nz,)),
            dma((nz, 2)),
            dma((nz,)),
            dma((nz,)),
            dma((nz,)),
            dma((nz,)),
            dma((rows, nz)),
            dma((4,)),
            dma((nz,)),
            dma((nz,)),
        ],
        compiler_params=pltpu.CompilerParams(
            collective_id=0, has_side_effects=True, vmem_limit_bytes=60 * 2**20
        ),
        cost_estimate=pl.CostEstimate(
            flops=2 * (rows + 2) * tok * out_weight.shape[0] * width,
            bytes_accessed=4 * out_weight.shape[0] * width,
            transcendentals=0,
        ),
    )(
        scene_lengths,
        bucket_ids,
        sensor_ids,
        gsd_ids,
        step_ids,
        jnp.transpose(qkv, (1, 0, 2)),
        out_weight,
        cotangent,
        step_table,
        gsd_table,
        sensor_table,
        bucket_table,
    )
    mixed, grad, total = pl.pallas_call(
        last_kernel,
        out_shape=(
            jax.ShapeDtypeStruct(mixed.shape, bf16),
            jax.ShapeDtypeStruct(grad.shape, bf16),
            jax.ShapeDtypeStruct(out_weight.shape, bf16),
        ),
        in_specs=[pl.BlockSpec(memory_space=pl.ANY)] * 5,
        out_specs=(pl.BlockSpec(memory_space=pl.ANY),) * 3,
        scratch_shapes=[
            pltpu.VMEM(mixed.shape, bf16),
            pltpu.VMEM(grad.shape, bf16),
            pltpu.VMEM(head.shape, bf16),
            pltpu.VMEM(tail.shape, bf16),
            pltpu.VMEM(gat_all.shape, bf16),
            pltpu.VMEM((late, 2, local, width), bf16),
            dma((3,)),
            dma((early, 2)),
            dma((late, 2)),
            dma((2,)),
            dma((nz, 2)),
        ],
        compiler_params=pltpu.CompilerParams(vmem_limit_bytes=60 * 2**20),
        cost_estimate=pl.CostEstimate(
            flops=2 * rows * tok * late * 2 * local * width,
            bytes_accessed=6 * out_weight.shape[0] * width,
            transcendentals=0,
        ),
    )(mixed, grad, head, tail, gat_all)
    return (mixed, jnp.transpose(grad, (1, 0, 2)), total)


def solution(mesh):
    planes = mesh.shape["row"] == 4 and mesh.shape["col"] == 8
    return jax.shard_map(
        fused_device if planes else on_device,
        mesh=mesh,
        in_specs=(
            P("row", None, "col"),
            P(None, "col"),
            P("row", "col"),
            P("row"),
            P("row"),
            P("row"),
            P("row"),
            P("row"),
            P(None, "col"),
            P(None, "col"),
            P(None, "col"),
            P(None, "col"),
        ),
        out_specs=(P("row", "col"), P("row", None, "col"), P(None, "col")),
        check_vma=False,
    )
```

```python
import jax
import jax.numpy as jnp
from jax import lax
from jax.experimental import pallas as pl
from jax.experimental.pallas import tpu as pltpu
from jax.sharding import PartitionSpec as P

HEAD = 128


def scene_of(lengths, count):
    ends = jnp.cumsum(lengths)
    places = jnp.arange(count)
    return jnp.sum((places[:, None] >= ends[None, :]).astype(jnp.int32), axis=1)


def lookup(ids, table):
    picks = (ids[:, None] == jnp.arange(table.shape[0])[None, :]).astype(table.dtype)
    return jnp.dot(picks, table, preferred_element_type=jnp.float32)


def attend(queries, keys, values, same):
    factor = HEAD ** (-0.5)
    scores = jnp.einsum("the,she->hts", queries, keys, preferred_element_type=jnp.float32) * factor
    scores = jnp.where(same[None], scores, -1e30)
    top = jnp.max(scores, axis=-1, keepdims=True)
    weights = jnp.exp(scores - top)
    probs = weights / jnp.sum(weights, axis=-1, keepdims=True)
    rounded = probs.astype(jnp.bfloat16)
    output = jnp.einsum("hts,she->the", rounded, values, preferred_element_type=jnp.float32).astype(
        jnp.bfloat16
    )
    return (probs, rounded, output)


def attend_back(queries, keys, values, probs, rounded, upstream):
    factor = HEAD ** (-0.5)
    grad_values = jnp.einsum(
        "hts,the->she", rounded, upstream, preferred_element_type=jnp.float32
    ).astype(jnp.bfloat16)
    grad_probs = jnp.einsum("the,she->hts", upstream, values, preferred_element_type=jnp.float32)
    inner = jnp.sum(probs * grad_probs, axis=-1, keepdims=True)
    grad_scores = (probs * (grad_probs - inner)).astype(jnp.bfloat16)
    grad_queries = (
        jnp.einsum("hts,she->the", grad_scores, keys, preferred_element_type=jnp.float32) * factor
    ).astype(jnp.bfloat16)
    grad_keys = (
        jnp.einsum("hts,the->she", grad_scores, queries, preferred_element_type=jnp.float32)
        * factor
    ).astype(jnp.bfloat16)
    stacked = jnp.stack([grad_queries, grad_keys, grad_values], axis=1)
    return stacked.reshape(stacked.shape[0], 3, stacked.shape[2] * stacked.shape[3])


def on_device(
    qkv,
    out_weight,
    cotangent,
    scene_lengths,
    bucket_ids,
    sensor_ids,
    gsd_ids,
    step_ids,
    step_table,
    gsd_table,
    sensor_table,
    bucket_table,
):
    tok_rows = qkv.shape[0]
    local_width = qkv.shape[2]
    heads_here = local_width // HEAD
    gate_scene = lookup(step_ids, step_table) + lookup(gsd_ids, gsd_table)
    gate_scene = gate_scene + lookup(sensor_ids, sensor_table) + lookup(bucket_ids, bucket_table)
    segments = scene_of(scene_lengths, tok_rows)
    member = (segments[:, None] == jnp.arange(scene_lengths.shape[0])[None, :]).astype(jnp.float32)
    gate = jnp.dot(
        member, gate_scene, precision=lax.Precision.HIGHEST, preferred_element_type=jnp.float32
    )
    same = segments[:, None] == segments[None, :]
    block = qkv.reshape(tok_rows, 3, heads_here, HEAD)
    queries = block[:, 0]
    keys = block[:, 1]
    values = block[:, 2]
    probs, rounded, attended = attend(queries, keys, values, same)
    attended = attended.reshape(tok_rows, local_width)
    rows = out_weight
    projected = jnp.dot(
        lax.all_gather(attended, "col", axis=1, tiled=True),
        rows,
        preferred_element_type=jnp.float32,
    )
    mixed = (gate * projected).astype(jnp.bfloat16)
    gated = (gate * cotangent.astype(jnp.float32)).astype(jnp.bfloat16)
    rows = out_weight
    summed = lax.psum_scatter(
        lax.dot_general(
            rows, gated, (((1,), (1,)), ((), ())), preferred_element_type=jnp.float32
        ).astype(jnp.bfloat16),
        "col",
        scatter_dimension=0,
        tiled=True,
    )
    upstream = summed.T.reshape(tok_rows, heads_here, HEAD)
    grad_qkv = attend_back(queries, keys, values, probs, rounded, upstream)
    partial_sum = lax.dot_general(
        lax.all_gather(attended, "col", axis=1, tiled=True),
        gated,
        (((0,), (0,)), ((), ())),
        preferred_element_type=jnp.float32,
    )
    total = lax.psum(partial_sum.astype(jnp.bfloat16), "row")
    return (mixed, grad_qkv, total)


def dot(a, b, dims):
    return lax.dot_general(a, b, (dims, ((), ())), preferred_element_type=jnp.float32)


def remote(src, dst, send, recv, device):
    return pltpu.make_async_remote_copy(
        src_ref=src,
        dst_ref=dst,
        send_sem=send,
        recv_sem=recv,
        device_id=device,
        device_id_type=pl.DeviceIdType.MESH,
    )


def origins_of(z, nz):
    orders = [sorted(range(nz), key=lambda o: (abs(o - p), o)) for p in range(nz)]
    origins = []
    for j in range(nz):
        picked = orders[0][j]
        for p in range(1, nz):
            picked = jnp.where(z == p, orders[p][j], picked)
        origins.append(picked)
    return origins


def last_kernel(
    mixed_in,
    grad_in,
    total_head,
    att_tail,
    gat_all,
    mixed_out,
    grad_out,
    total_out,
    mixed,
    grad,
    head,
    att,
    gat,
    tail,
    in_sem,
    head_sem,
    att_sem,
    out_sem,
    total_sem,
):
    early, parts, local, width = head.shape
    late = att.shape[0]
    origins = origins_of(lax.axis_index("col") // 2, early + late)

    def place(j, c):
        return total_out.at[pl.ds(pl.multiple_of((2 * origins[j] + c) * local, local), local)]

    gat_load = pltpu.make_async_copy(gat_all, gat, in_sem.at[0])
    gat_load.start()
    att_loads = {}
    for j in range(late):
        for c in range(parts):
            att_loads[j, c] = pltpu.make_async_copy(att_tail.at[j, c], att.at[j, c], att_sem.at[j, c])
            att_loads[j, c].start()
    moves = []
    for j in range(early):
        for c in range(parts):
            moves.append((
                pltpu.make_async_copy(total_head.at[j, c], head.at[j, c], head_sem.at[j, c]),
                pltpu.make_async_copy(head.at[j, c], place(j, c), total_sem.at[j, c]),
            ))
    moves.append((
        pltpu.make_async_copy(mixed_in, mixed, in_sem.at[1]),
        pltpu.make_async_copy(mixed, mixed_out, out_sem.at[0]),
    ))
    moves.append((
        pltpu.make_async_copy(grad_in, grad, in_sem.at[2]),
        pltpu.make_async_copy(grad, grad_out, out_sem.at[1]),
    ))
    for load, store in moves:
        load.start()
    gat_load.wait()
    steps = late * parts
    share = -(-len(moves) // steps)
    stores = []
    for i in range(steps):
        j, c = divmod(i, parts)
        att_loads[j, c].wait()
        tail[j, c] = dot(att[j, c], gat[...], ((0,), (0,))).astype(jnp.bfloat16)
        stores.append(pltpu.make_async_copy(tail.at[j, c], place(early + j, c), total_sem.at[early + j, c]))
        stores[-1].start()
        for load, store in moves[i * share : (i + 1) * share]:
            load.wait()
            store.start()
            stores.append(store)
    for store in stores:
        store.wait()


def fused_kernel(
    lengths,
    bucket_ids,
    sensor_ids,
    gsd_ids,
    step_ids,
    qkv,
    weight_hbm,
    cotangent,
    step_hbm,
    gsd_table,
    sensor_table,
    bucket_table,
    mixed_out,
    grad_out,
    total_head,
    att_tail,
    gat_all,
    step_table,
    weight,
    att,
    gat,
    gate,
    total_acc,
    probs_s,
    own,
    pair_send,
    pair_recv,
    line_send,
    line_recv,
    upstream,
    w_sem,
    step_sem,
    out_sem,
    tail_sem,
    gat_sem,
    att_recv,
    gat_recv,
    pr_recv,
    lr_recv,
    z_sent,
    x_sent,
    y_sent,
    fx_sent,
    fy_sent,
    p_sent,
    g_sent,
    ps_sent,
    ls_sent,
):
    tok, width = cotangent.shape
    local = qkv.shape[2]
    heads = local // HEAD
    half = tok // 2
    nb = weight.shape[0]
    nz = nb // 2
    scenes = lengths.shape[0]
    early = total_head.shape[0]
    factor = HEAD ** (-0.5)
    r = lax.axis_index("row")
    col = lax.axis_index("col")
    z = col // 2
    k = lax.rem(col, 2)
    xn = r + 1 - 2 * lax.rem(r, 2)
    yn = lax.rem(r + 2, 4)
    dn = 3 - r
    pair = {"col": col + 1 - 2 * k}
    to_x = {"row": xn}
    to_y = {"row": yn}

    barrier = pltpu.get_barrier_semaphore()
    peers = [pair, to_x, to_y] + [{"col": 2 * lax.rem(z + d, nz) + k} for d in range(1, nz)]
    for peer in peers:
        pl.semaphore_signal(
            barrier, inc=1, device_id=peer, device_id_type=pl.DeviceIdType.MESH
        )
    pl.semaphore_wait(barrier, len(peers))

    def load(b):
        return pltpu.make_async_copy(
            weight_hbm.at[pl.ds(b * local, local)], weight.at[b], w_sem.at[b]
        )

    step_load = pltpu.make_async_copy(step_hbm, step_table, step_sem)
    step_load.start()
    for b in range(nb):
        load(b).start()

    def token_rows(row, part=None):
        if part is None:
            return pl.ds(pl.multiple_of(row * tok, tok), tok)
        return pl.ds(pl.multiple_of(row * tok + part * half, half), half)

    place_col = lax.broadcasted_iota(jnp.int32, (tok, 1), 0)
    place_row = lax.broadcasted_iota(jnp.int32, (1, tok), 1)
    seg_col = jnp.zeros((tok, 1), jnp.int32)
    seg_row = jnp.zeros((1, tok), jnp.int32)
    end = 0
    for s in range(scenes):
        end = end + lengths[s]
        seg_col = seg_col + (place_col >= end).astype(jnp.int32)
        seg_row = seg_row + (place_row >= end).astype(jnp.int32)

    same = seg_col == seg_row
    mine = 2 * z + k
    for h in range(heads):
        lanes = slice(h * HEAD, (h + 1) * HEAD)
        scores = dot(qkv[0, :, lanes], qkv[1, :, lanes], ((1,), (1,))) * factor
        scores = jnp.where(same, scores, -1e30)
        top = jnp.max(scores, axis=-1, keepdims=True)
        weights = jnp.exp(scores - top)
        probs = weights / jnp.sum(weights, axis=-1, keepdims=True)
        probs_s[h] = probs
        out = dot(probs.astype(jnp.bfloat16), qkv[2, :, lanes], ((1,), (0,)))
        att[mine, token_rows(r), lanes] = out.astype(jnp.bfloat16)

    origins = origins_of(z, nz)

    def block(row, b, part=None):
        return att.at[b, token_rows(row, part)]

    def att_copy(row, b, part, send, device):
        ref = block(row, b, part)
        return remote(ref, ref, send, att_recv.at[row, b, 0 if part is None else part], device)

    def pass_on(row, o):
        return att_copy(row, 2 * o + k, None, p_sent.at[row, o], pair)

    def got(row, b, part=None):
        att_copy(row, b, part, p_sent.at[0, 0], pair).wait_recv()

    def upward(which, o):
        row = dn if which else r
        return att_copy(
            row, 2 * o + k, None, z_sent.at[which, o, 0], {"col": lax.rem(col + 2, 2 * nz)}
        )

    def downward(which, o):
        row = dn if which else r
        return att_copy(
            row, 2 * o + k, None, z_sent.at[which, o, 1], {"col": lax.rem(col + 2 * nz - 2, 2 * nz)}
        )

    def along_z(which, o):
        @pl.when((o <= z) & (z < nz - 1))
        def _():
            upward(which, o).start()

        @pl.when((o >= z) & (z > 0))
        def _():
            downward(which, o).start()

    def stage_a(j):
        o = origins[j]
        if j > 0:
            got(r, 2 * o + k)
        along_z(0, o)
        att_copy(r, 2 * o + k, None, x_sent.at[j], to_x).start()
        att_copy(r, 2 * o + k, None, y_sent.at[j], to_y).start()
        pass_on(r, o).start()

    def stage_b(j):
        o = origins[j]
        b = 2 * o + k
        got(xn, b)
        if j == 0:
            att_copy(xn, b, 0, fy_sent.at[j], to_y).start()
        pass_on(xn, o).start()
        got(yn, b)
        if j == 0:
            att_copy(yn, b, 1, fx_sent.at[j], to_x).start()
        pass_on(yn, o).start()

    def stage_c(j):
        o = origins[j]
        if j == 0:
            got(dn, 2 * o + k, 0)
            got(dn, 2 * o + k, 1)
        else:
            got(dn, 2 * o + k)
        along_z(1, o)
        pass_on(dn, o).start()

    def stage_m(j):
        o = origins[j]
        got(r, 2 * o + 1 - k)

        def add(c, carry):
            b = 2 * o + c
            term = dot(att[b, token_rows(r), :], weight[b], ((1,), (0,)))
            if j == 0:
                total_acc[c] = term
            else:
                total_acc[c] += term
            return carry

        lax.fori_loop(0, 2, add, 0)

    def out_copy(j, c):
        return pltpu.make_async_copy(
            weight.at[2 * origins[j] + c], total_head.at[j, c], out_sem.at[j, c]
        )

    def tail_copy(j, c):
        return pltpu.make_async_copy(
            att.at[2 * origins[j] + c], att_tail.at[j - early, c], tail_sem.at[j - early, c]
        )

    gat_out = pltpu.make_async_copy(gat, gat_all, gat_sem)

    def stage_w(j):
        o = origins[j]
        for row in (xn, yn, dn):
            got(row, 2 * o + 1 - k)

        def form(c, carry):
            b = 2 * o + c
            weight[b] = dot(att[b], gat[...], ((0,), (0,))).astype(jnp.bfloat16)
            out_copy(j, c).start()
            return carry

        if j < early:
            lax.fori_loop(0, 2, form, 0)
        else:
            for c in range(2):
                tail_copy(j, c).start()

    stage_a(0)

    def picks(ids, table):
        count = table.shape[0]
        which = lax.broadcasted_iota(jnp.int32, (scenes, count), 0)
        place = lax.broadcasted_iota(jnp.int32, (scenes, count), 1)
        wanted = jnp.zeros((scenes, count), jnp.int32)
        for s in range(scenes):
            wanted = jnp.where(which == s, ids[s], wanted)
        chosen = jnp.where(place == wanted, 1.0, 0.0).astype(table.dtype)
        return dot(chosen, table[...], ((1,), (0,)))

    step_load.wait()
    gate_scene = picks(step_ids, step_table) + picks(gsd_ids, gsd_table)
    gate_scene = gate_scene + picks(sensor_ids, sensor_table) + picks(bucket_ids, bucket_table)
    value = jnp.broadcast_to(gate_scene[0:1, :], (tok, width))
    for s in range(1, scenes):
        value = jnp.where(seg_col == s, gate_scene[s : s + 1, :], value)
    gate[...] = value
    gat[token_rows(r), :] = (value * cotangent[...].astype(jnp.float32)).astype(jnp.bfloat16)

    def gat_copy(row, part, send, device):
        rows = gat.at[token_rows(row, part)]
        return remote(rows, rows, g_sent.at[send], gat_recv.at[row, 0 if part is None else part], device)

    gat_copy(r, None, 0, to_x).start()
    gat_copy(r, None, 1, to_y).start()

    for b in range(nb):
        load(b).wait()

    def pair_copy(t):
        return remote(pair_send.at[t], pair_recv.at[t], ps_sent.at[t], pr_recv.at[t], pair)

    def part_of(b):
        return dot(gat[token_rows(r), :], weight[b], ((1,), (1,)))

    def for_pair(i, carry):
        t = lax.rem(z + 1 + i, nz)
        pair_send[t] = part_of(2 * t + 1 - k).astype(jnp.bfloat16)
        pair_copy(t).start()
        return carry

    lax.fori_loop(0, nz, for_pair, 0)

    def for_self(i, carry):
        t = lax.rem(z + 1 + i, nz)
        own[t] = part_of(2 * t + k)
        return carry

    lax.fori_loop(0, nz, for_self, 0)

    for t in range(nz):
        pair_copy(t).wait_recv()

    def line_copy(t, down, device):
        slot = t + nz if down else t
        return remote(
            line_send.at[t], line_recv.at[slot], ls_sent.at[t], lr_recv.at[slot], device
        )

    def hop(p, t):
        down = t < p
        summed = own[t] + pair_recv[t].astype(jnp.float32)
        if 0 < p < nz - 1:
            line_copy(t, down, pair).wait_recv()
            summed = summed + line_recv[t + nz if down else t].astype(jnp.float32)
        line_send[t] = summed.astype(jnp.bfloat16)
        to = col - 2 if down else col + 2
        line_copy(t, down, {"col": lax.rem(to + 2 * nz, 2 * nz)}).start()

    def line_step(tau):
        for p in range(nz):
            turns = []
            for t in range(nz):
                if t == p:
                    continue
                near, far = (p, t) if t > p else (nz - 1 - p, nz - 1 - t)
                turn = 0 if near == 0 else nz - 1 - far + near
                if turn == tau:
                    turns.append((-far, t))
            if turns:

                @pl.when(z == p)
                def _():
                    for _, t in sorted(turns):
                        hop(p, t)

    line_step(0)
    stage_b(0)
    stage_a(1)
    line_step(1)
    stage_c(0)
    stage_m(0)
    stage_a(2)
    line_step(2)
    gat_copy(xn, None, 0, to_x).wait_recv()
    gat_copy(xn, 0, 2, to_y).start()
    gat_copy(yn, None, 0, to_x).wait_recv()
    gat_copy(yn, 1, 3, to_x).start()
    stage_a(3)
    stage_b(1)
    stage_c(1)
    stage_m(1)
    gat_copy(dn, 0, 0, to_x).wait_recv()
    gat_copy(dn, 1, 0, to_x).wait_recv()
    gat_out.start()
    stage_w(0)

    own[z] = own[z] + pair_recv[z].astype(jnp.float32)

    @pl.when(z > 0)
    def _():
        line_copy(z, False, pair).wait_recv()
        own[z] = own[z] + line_recv[z].astype(jnp.float32)

    @pl.when(z < nz - 1)
    def _():
        line_copy(z, True, pair).wait_recv()
        own[z] = own[z] + line_recv[nz + z].astype(jnp.float32)

    upstream[...] = own[z].astype(jnp.bfloat16)
    for h in range(heads):
        lanes = slice(h * HEAD, (h + 1) * HEAD)
        upper = upstream[:, lanes]
        probs = probs_s[h]
        grad_out[2, :, lanes] = dot(probs.astype(jnp.bfloat16), upper, ((0,), (0,))).astype(
            jnp.bfloat16
        )
        grad_probs = dot(upper, qkv[2, :, lanes], ((1,), (1,)))
        inner = jnp.sum(probs * grad_probs, axis=-1, keepdims=True)
        grad_scores = (probs * (grad_probs - inner)).astype(jnp.bfloat16)
        grad_out[0, :, lanes] = (
            dot(grad_scores, qkv[1, :, lanes], ((1,), (0,))) * factor
        ).astype(jnp.bfloat16)
        grad_out[1, :, lanes] = (
            dot(grad_scores, qkv[0, :, lanes], ((0,), (0,))) * factor
        ).astype(jnp.bfloat16)

    stage_b(2)
    stage_m(2)
    stage_m(3)
    mixed_out[...] = (gate[...] * (total_acc[0] + total_acc[1])).astype(jnp.bfloat16)
    stage_c(2)
    stage_w(1)
    stage_b(3)
    stage_w(2)
    stage_c(3)
    stage_w(3)

    gat_copy(r, None, 0, to_x).wait_send()
    gat_copy(r, None, 1, to_y).wait_send()
    gat_copy(xn, 0, 2, to_y).wait_send()
    gat_copy(yn, 1, 3, to_x).wait_send()
    for j in range(nz):
        o = origins[j]
        b = 2 * o + k

        @pl.when((o <= z) & (z < nz - 1))
        def _():
            upward(0, o).wait_send()
            upward(1, o).wait_send()

        @pl.when((o >= z) & (z > 0))
        def _():
            downward(0, o).wait_send()
            downward(1, o).wait_send()

        att_copy(r, b, None, x_sent.at[j], to_x).wait_send()
        att_copy(r, b, None, y_sent.at[j], to_y).wait_send()
        if j == 0:
            att_copy(xn, b, 0, fy_sent.at[j], to_y).wait_send()
            att_copy(yn, b, 1, fx_sent.at[j], to_x).wait_send()
        for row in (r, xn, yn, dn):
            pass_on(row, o).wait_send()
        pair_copy(j).wait_send()
        for c in range(2):
            (out_copy if j < early else tail_copy)(j, c).wait()
    for d in range(1, nz):
        line_copy(lax.rem(z + d, nz), False, pair).wait_send()
    gat_out.wait()


def fused_device(
    qkv,
    out_weight,
    cotangent,
    scene_lengths,
    bucket_ids,
    sensor_ids,
    gsd_ids,
    step_ids,
    step_table,
    gsd_table,
    sensor_table,
    bucket_table,
):
    rows = lax.axis_size("row")
    cols = lax.axis_size("col")
    nz = cols // 2
    tok, width = cotangent.shape
    local = qkv.shape[2]
    early = nz - 1
    late = nz - early
    dma = pltpu.SemaphoreType.DMA
    bf16 = jnp.bfloat16
    mixed, grad, head, tail, gat_all = pl.pallas_call(
        fused_kernel,
        out_shape=(
            jax.ShapeDtypeStruct((tok, width), bf16),
            jax.ShapeDtypeStruct((3, tok, local), bf16),
            jax.ShapeDtypeStruct((early, 2, local, width), bf16),
            jax.ShapeDtypeStruct((late, 2, rows * tok, local), bf16),
            jax.ShapeDtypeStruct((rows * tok, width), bf16),
        ),
        in_specs=[pl.BlockSpec(memory_space=pltpu.SMEM)] * 5
        + [
            pl.BlockSpec(memory_space=pltpu.VMEM),
            pl.BlockSpec(memory_space=pl.ANY),
            pl.BlockSpec(memory_space=pltpu.VMEM),
            pl.BlockSpec(memory_space=pl.ANY),
        ]
        + [pl.BlockSpec(memory_space=pltpu.VMEM)] * 3,
        out_specs=(pl.BlockSpec(memory_space=pltpu.VMEM),) * 2
        + (pl.BlockSpec(memory_space=pl.ANY),) * 3,
        scratch_shapes=[
            pltpu.VMEM(step_table.shape, bf16),
            pltpu.VMEM((cols, local, width), bf16),
            pltpu.VMEM((cols, rows * tok, local), bf16),
            pltpu.VMEM((rows * tok, width), bf16),
            pltpu.VMEM((tok, width), jnp.float32),
            pltpu.VMEM((2, tok, width), jnp.float32),
            pltpu.VMEM((local // HEAD, tok, tok), jnp.float32),
            pltpu.VMEM((nz, tok, local), jnp.float32),
            pltpu.VMEM((nz, tok, local), bf16),
            pltpu.VMEM((nz, tok, local), bf16),
            pltpu.VMEM((nz, tok, local), bf16),
            pltpu.VMEM((2 * nz, tok, local), bf16),
            pltpu.VMEM((tok, local), bf16),
            dma((cols,)),
            dma,
            dma((early, 2)),
            dma((late, 2)),
            dma,
            dma((rows, cols, 2)),
            dma((rows, 2)),
            dma((nz,)),
            dma((2 * nz,)),
            dma((2, nz, 2)),
            dma((nz,)),
            dma((nz,)),
            dma((nz,)),
            dma((nz,)),
            dma((rows, nz)),
            dma((4,)),
            dma((nz,)),
            dma((nz,)),
        ],
        compiler_params=pltpu.CompilerParams(
            collective_id=0, has_side_effects=True, vmem_limit_bytes=60 * 2**20
        ),
        cost_estimate=pl.CostEstimate(
            flops=2 * (rows + 2) * tok * out_weight.shape[0] * width,
            bytes_accessed=4 * out_weight.shape[0] * width,
            transcendentals=0,
        ),
    )(
        scene_lengths,
        bucket_ids,
        sensor_ids,
        gsd_ids,
        step_ids,
        jnp.transpose(qkv, (1, 0, 2)),
        out_weight,
        cotangent,
        step_table,
        gsd_table,
        sensor_table,
        bucket_table,
    )
    mixed, grad, total = pl.pallas_call(
        last_kernel,
        out_shape=(
            jax.ShapeDtypeStruct(mixed.shape, bf16),
            jax.ShapeDtypeStruct(grad.shape, bf16),
            jax.ShapeDtypeStruct(out_weight.shape, bf16),
        ),
        in_specs=[pl.BlockSpec(memory_space=pl.ANY)] * 5,
        out_specs=(pl.BlockSpec(memory_space=pl.ANY),) * 3,
        scratch_shapes=[
            pltpu.VMEM(mixed.shape, bf16),
            pltpu.VMEM(grad.shape, bf16),
            pltpu.VMEM(head.shape, bf16),
            pltpu.VMEM(tail.shape, bf16),
            pltpu.VMEM(gat_all.shape, bf16),
            pltpu.VMEM((late, 2, local, width), bf16),
            dma((3,)),
            dma((early, 2)),
            dma((late, 2)),
            dma((2,)),
            dma((nz, 2)),
        ],
        compiler_params=pltpu.CompilerParams(vmem_limit_bytes=60 * 2**20),
        cost_estimate=pl.CostEstimate(
            flops=2 * rows * tok * late * 2 * local * width,
            bytes_accessed=6 * out_weight.shape[0] * width,
            transcendentals=0,
        ),
    )(mixed, grad, head, tail, gat_all)
    return (mixed, jnp.transpose(grad, (1, 0, 2)), total)


def solution(mesh):
    planes = mesh.shape["row"] == 4 and mesh.shape["col"] == 8
    return jax.shard_map(
        fused_device if planes else on_device,
        mesh=mesh,
        in_specs=(
            P("row", None, "col"),
            P(None, "col"),
            P("row", "col"),
            P("row"),
            P("row"),
            P("row"),
            P("row"),
            P("row"),
            P(None, "col"),
            P(None, "col"),
            P(None, "col"),
            P(None, "col"),
        ),
        out_specs=(P("row", "col"), P("row", None, "col"), P(None, "col")),
        check_vma=False,
    )
```

```python
import jax
import jax.numpy as jnp
from jax import lax
from jax.experimental import pallas as pl
from jax.experimental.pallas import tpu as pltpu
from jax.sharding import PartitionSpec as P

HEAD = 128


def scene_of(lengths, count):
    ends = jnp.cumsum(lengths)
    places = jnp.arange(count)
    return jnp.sum((places[:, None] >= ends[None, :]).astype(jnp.int32), axis=1)


def lookup(ids, table):
    picks = (ids[:, None] == jnp.arange(table.shape[0])[None, :]).astype(table.dtype)
    return jnp.dot(picks, table, preferred_element_type=jnp.float32)


def attend(queries, keys, values, same):
    factor = HEAD ** (-0.5)
    scores = jnp.einsum("the,she->hts", queries, keys, preferred_element_type=jnp.float32) * factor
    scores = jnp.where(same[None], scores, -1e30)
    top = jnp.max(scores, axis=-1, keepdims=True)
    weights = jnp.exp(scores - top)
    probs = weights / jnp.sum(weights, axis=-1, keepdims=True)
    rounded = probs.astype(jnp.bfloat16)
    output = jnp.einsum("hts,she->the", rounded, values, preferred_element_type=jnp.float32).astype(
        jnp.bfloat16
    )
    return (probs, rounded, output)


def attend_back(queries, keys, values, probs, rounded, upstream):
    factor = HEAD ** (-0.5)
    grad_values = jnp.einsum(
        "hts,the->she", rounded, upstream, preferred_element_type=jnp.float32
    ).astype(jnp.bfloat16)
    grad_probs = jnp.einsum("the,she->hts", upstream, values, preferred_element_type=jnp.float32)
    inner = jnp.sum(probs * grad_probs, axis=-1, keepdims=True)
    grad_scores = (probs * (grad_probs - inner)).astype(jnp.bfloat16)
    grad_queries = (
        jnp.einsum("hts,she->the", grad_scores, keys, preferred_element_type=jnp.float32) * factor
    ).astype(jnp.bfloat16)
    grad_keys = (
        jnp.einsum("hts,the->she", grad_scores, queries, preferred_element_type=jnp.float32)
        * factor
    ).astype(jnp.bfloat16)
    stacked = jnp.stack([grad_queries, grad_keys, grad_values], axis=1)
    return stacked.reshape(stacked.shape[0], 3, stacked.shape[2] * stacked.shape[3])


def on_device(
    qkv,
    out_weight,
    cotangent,
    scene_lengths,
    bucket_ids,
    sensor_ids,
    gsd_ids,
    step_ids,
    step_table,
    gsd_table,
    sensor_table,
    bucket_table,
):
    tok_rows = qkv.shape[0]
    local_width = qkv.shape[2]
    heads_here = local_width // HEAD
    gate_scene = lookup(step_ids, step_table) + lookup(gsd_ids, gsd_table)
    gate_scene = gate_scene + lookup(sensor_ids, sensor_table) + lookup(bucket_ids, bucket_table)
    segments = scene_of(scene_lengths, tok_rows)
    member = (segments[:, None] == jnp.arange(scene_lengths.shape[0])[None, :]).astype(jnp.float32)
    gate = jnp.dot(
        member, gate_scene, precision=lax.Precision.HIGHEST, preferred_element_type=jnp.float32
    )
    same = segments[:, None] == segments[None, :]
    block = qkv.reshape(tok_rows, 3, heads_here, HEAD)
    queries = block[:, 0]
    keys = block[:, 1]
    values = block[:, 2]
    probs, rounded, attended = attend(queries, keys, values, same)
    attended = attended.reshape(tok_rows, local_width)
    rows = out_weight
    projected = jnp.dot(
        lax.all_gather(attended, "col", axis=1, tiled=True),
        rows,
        preferred_element_type=jnp.float32,
    )
    mixed = (gate * projected).astype(jnp.bfloat16)
    gated = (gate * cotangent.astype(jnp.float32)).astype(jnp.bfloat16)
    rows = out_weight
    summed = lax.psum_scatter(
        lax.dot_general(
            rows, gated, (((1,), (1,)), ((), ())), preferred_element_type=jnp.float32
        ).astype(jnp.bfloat16),
        "col",
        scatter_dimension=0,
        tiled=True,
    )
    upstream = summed.T.reshape(tok_rows, heads_here, HEAD)
    grad_qkv = attend_back(queries, keys, values, probs, rounded, upstream)
    partial_sum = lax.dot_general(
        lax.all_gather(attended, "col", axis=1, tiled=True),
        gated,
        (((0,), (0,)), ((), ())),
        preferred_element_type=jnp.float32,
    )
    total = lax.psum(partial_sum.astype(jnp.bfloat16), "row")
    return (mixed, grad_qkv, total)


def dot(a, b, dims):
    return lax.dot_general(a, b, (dims, ((), ())), preferred_element_type=jnp.float32)


def remote(src, dst, send, recv, device):
    return pltpu.make_async_remote_copy(
        src_ref=src,
        dst_ref=dst,
        send_sem=send,
        recv_sem=recv,
        device_id=device,
        device_id_type=pl.DeviceIdType.MESH,
    )


def origins_of(z, nz):
    orders = [
        sorted(range(nz), key=lambda o: (abs(o - p), -o if 2 * p < nz else o)) for p in range(nz)
    ]
    origins = []
    for j in range(nz):
        picked = orders[0][j]
        for p in range(1, nz):
            picked = jnp.where(z == p, orders[p][j], picked)
        origins.append(picked)
    return origins


def last_kernel(
    mixed_in,
    grad_in,
    total_head,
    att_tail,
    gat_all,
    mixed_out,
    grad_out,
    total_out,
    mixed,
    grad,
    head,
    att,
    gat,
    tail,
    in_sem,
    head_sem,
    att_sem,
    out_sem,
    total_sem,
):
    early, parts, local, width = head.shape
    late = att.shape[0]
    origins = origins_of(lax.axis_index("col") // 2, early + late)

    def place(j, c):
        return total_out.at[pl.ds(pl.multiple_of((2 * origins[j] + c) * local, local), local)]

    gat_load = pltpu.make_async_copy(gat_all, gat, in_sem.at[0])
    gat_load.start()
    att_loads = {}
    for j in range(late):
        for c in range(parts):
            att_loads[j, c] = pltpu.make_async_copy(att_tail.at[j, c], att.at[j, c], att_sem.at[j, c])
            att_loads[j, c].start()
    moves = []
    for j in range(early):
        for c in range(parts):
            moves.append((
                pltpu.make_async_copy(total_head.at[j, c], head.at[j, c], head_sem.at[j, c]),
                pltpu.make_async_copy(head.at[j, c], place(j, c), total_sem.at[j, c]),
            ))
    moves.append((
        pltpu.make_async_copy(mixed_in, mixed, in_sem.at[1]),
        pltpu.make_async_copy(mixed, mixed_out, out_sem.at[0]),
    ))
    moves.append((
        pltpu.make_async_copy(grad_in, grad, in_sem.at[2]),
        pltpu.make_async_copy(grad, grad_out, out_sem.at[1]),
    ))
    for load, store in moves:
        load.start()
    gat_load.wait()
    steps = late * parts
    share = -(-len(moves) // steps)
    stores = []
    for i in range(steps):
        j, c = divmod(i, parts)
        att_loads[j, c].wait()
        tail[j, c] = dot(att[j, c], gat[...], ((0,), (0,))).astype(jnp.bfloat16)
        stores.append(pltpu.make_async_copy(tail.at[j, c], place(early + j, c), total_sem.at[early + j, c]))
        stores[-1].start()
        for load, store in moves[i * share : (i + 1) * share]:
            load.wait()
            store.start()
            stores.append(store)
    for store in stores:
        store.wait()


def fused_kernel(
    lengths,
    bucket_ids,
    sensor_ids,
    gsd_ids,
    step_ids,
    qkv,
    weight_hbm,
    cotangent,
    step_hbm,
    gsd_table,
    sensor_table,
    bucket_table,
    mixed_out,
    grad_out,
    total_head,
    att_tail,
    gat_all,
    step_table,
    weight,
    att,
    gat,
    gate,
    total_acc,
    probs_s,
    own,
    pair_send,
    pair_recv,
    line_send,
    line_recv,
    upstream,
    w_sem,
    step_sem,
    out_sem,
    tail_sem,
    gat_sem,
    att_recv,
    gat_recv,
    pr_recv,
    lr_recv,
    z_sent,
    x_sent,
    y_sent,
    fx_sent,
    fy_sent,
    p_sent,
    g_sent,
    ps_sent,
    ls_sent,
):
    tok, width = cotangent.shape
    local = qkv.shape[2]
    heads = local // HEAD
    half = tok // 2
    nb = weight.shape[0]
    nz = nb // 2
    scenes = lengths.shape[0]
    early = total_head.shape[0]
    factor = HEAD ** (-0.5)
    r = lax.axis_index("row")
    col = lax.axis_index("col")
    z = col // 2
    k = lax.rem(col, 2)
    xn = r + 1 - 2 * lax.rem(r, 2)
    yn = lax.rem(r + 2, 4)
    dn = 3 - r
    pair = {"col": col + 1 - 2 * k}
    to_x = {"row": xn}
    to_y = {"row": yn}

    barrier = pltpu.get_barrier_semaphore()
    peers = [pair, to_x, to_y] + [{"col": 2 * lax.rem(z + d, nz) + k} for d in range(1, nz)]
    for peer in peers:
        pl.semaphore_signal(
            barrier, inc=1, device_id=peer, device_id_type=pl.DeviceIdType.MESH
        )
    pl.semaphore_wait(barrier, len(peers))

    def load(b):
        return pltpu.make_async_copy(
            weight_hbm.at[pl.ds(b * local, local)], weight.at[b], w_sem.at[b]
        )

    step_load = pltpu.make_async_copy(step_hbm, step_table, step_sem)
    step_load.start()
    for b in range(nb):
        load(b).start()

    def token_rows(row, part=None):
        if part is None:
            return pl.ds(pl.multiple_of(row * tok, tok), tok)
        return pl.ds(pl.multiple_of(row * tok + part * half, half), half)

    place_col = lax.broadcasted_iota(jnp.int32, (tok, 1), 0)
    place_row = lax.broadcasted_iota(jnp.int32, (1, tok), 1)
    seg_col = jnp.zeros((tok, 1), jnp.int32)
    seg_row = jnp.zeros((1, tok), jnp.int32)
    end = 0
    for s in range(scenes):
        end = end + lengths[s]
        seg_col = seg_col + (place_col >= end).astype(jnp.int32)
        seg_row = seg_row + (place_row >= end).astype(jnp.int32)

    same = seg_col == seg_row
    mine = 2 * z + k
    for h in range(heads):
        lanes = slice(h * HEAD, (h + 1) * HEAD)
        scores = dot(qkv[0, :, lanes], qkv[1, :, lanes], ((1,), (1,))) * factor
        scores = jnp.where(same, scores, -1e30)
        top = jnp.max(scores, axis=-1, keepdims=True)
        weights = jnp.exp(scores - top)
        probs = weights / jnp.sum(weights, axis=-1, keepdims=True)
        probs_s[h] = probs
        out = dot(probs.astype(jnp.bfloat16), qkv[2, :, lanes], ((1,), (0,)))
        att[mine, token_rows(r), lanes] = out.astype(jnp.bfloat16)

    origins = origins_of(z, nz)

    def block(row, b, part=None):
        return att.at[b, token_rows(row, part)]

    def att_copy(row, b, part, send, device):
        ref = block(row, b, part)
        return remote(ref, ref, send, att_recv.at[row, b, 0 if part is None else part], device)

    def pass_on(row, o):
        return att_copy(row, 2 * o + k, None, p_sent.at[row, o], pair)

    def got(row, b, part=None):
        att_copy(row, b, part, p_sent.at[0, 0], pair).wait_recv()

    def upward(which, o):
        row = dn if which else r
        return att_copy(
            row, 2 * o + k, None, z_sent.at[which, o, 0], {"col": lax.rem(col + 2, 2 * nz)}
        )

    def downward(which, o):
        row = dn if which else r
        return att_copy(
            row, 2 * o + k, None, z_sent.at[which, o, 1], {"col": lax.rem(col + 2 * nz - 2, 2 * nz)}
        )

    def along_z(which, o):
        @pl.when((o <= z) & (z < nz - 1))
        def _():
            upward(which, o).start()

        @pl.when((o >= z) & (z > 0))
        def _():
            downward(which, o).start()

    def stage_a(j):
        o = origins[j]
        if j > 0:
            got(r, 2 * o + k)
        along_z(0, o)
        pass_on(r, o).start()

    def over_plane(j):
        o = origins[j]
        att_copy(r, 2 * o + k, None, x_sent.at[j], to_x).start()
        att_copy(r, 2 * o + k, None, y_sent.at[j], to_y).start()

    def stage_b(j):
        o = origins[j]
        b = 2 * o + k
        got(xn, b)
        if j == 0:
            att_copy(xn, b, 0, fy_sent.at[j], to_y).start()
        pass_on(xn, o).start()
        got(yn, b)
        if j == 0:
            att_copy(yn, b, 1, fx_sent.at[j], to_x).start()
        pass_on(yn, o).start()

    def stage_c(j):
        o = origins[j]
        if j == 0:
            got(dn, 2 * o + k, 0)
            got(dn, 2 * o + k, 1)
        else:
            got(dn, 2 * o + k)
        along_z(1, o)
        pass_on(dn, o).start()

    def stage_m(j):
        o = origins[j]
        got(r, 2 * o + 1 - k)

        def add(c, carry):
            b = 2 * o + c
            term = dot(att[b, token_rows(r), :], weight[b], ((1,), (0,)))
            if j == 0:
                total_acc[c] = term
            else:
                total_acc[c] += term
            return carry

        lax.fori_loop(0, 2, add, 0)

    def out_copy(j, c):
        return pltpu.make_async_copy(
            weight.at[2 * origins[j] + c], total_head.at[j, c], out_sem.at[j, c]
        )

    def tail_copy(j, c):
        return pltpu.make_async_copy(
            att.at[2 * origins[j] + c], att_tail.at[j - early, c], tail_sem.at[j - early, c]
        )

    gat_out = pltpu.make_async_copy(gat, gat_all, gat_sem)

    def stage_w(j):
        o = origins[j]
        for row in (xn, yn, dn):
            got(row, 2 * o + 1 - k)

        def form(c, carry):
            b = 2 * o + c
            weight[b] = dot(att[b], gat[...], ((0,), (0,))).astype(jnp.bfloat16)
            out_copy(j, c).start()
            return carry

        if j < early:
            lax.fori_loop(0, 2, form, 0)
        else:
            for c in range(2):
                tail_copy(j, c).start()

    over_plane(0)
    stage_a(0)

    def picks(ids, table):
        count = table.shape[0]
        which = lax.broadcasted_iota(jnp.int32, (scenes, count), 0)
        place = lax.broadcasted_iota(jnp.int32, (scenes, count), 1)
        wanted = jnp.zeros((scenes, count), jnp.int32)
        for s in range(scenes):
            wanted = jnp.where(which == s, ids[s], wanted)
        chosen = jnp.where(place == wanted, 1.0, 0.0).astype(table.dtype)
        return dot(chosen, table[...], ((1,), (0,)))

    step_load.wait()
    gate_scene = picks(step_ids, step_table) + picks(gsd_ids, gsd_table)
    gate_scene = gate_scene + picks(sensor_ids, sensor_table) + picks(bucket_ids, bucket_table)
    value = jnp.broadcast_to(gate_scene[0:1, :], (tok, width))
    for s in range(1, scenes):
        value = jnp.where(seg_col == s, gate_scene[s : s + 1, :], value)
    gate[...] = value
    gat[token_rows(r), :] = (value * cotangent[...].astype(jnp.float32)).astype(jnp.bfloat16)

    def gat_copy(row, part, send, device):
        rows = gat.at[token_rows(row, part)]
        return remote(rows, rows, g_sent.at[send], gat_recv.at[row, 0 if part is None else part], device)


    for b in range(nb):
        load(b).wait()

    def pair_copy(t):
        return remote(pair_send.at[t], pair_recv.at[t], ps_sent.at[t], pr_recv.at[t], pair)

    def part_of(b):
        return dot(gat[token_rows(r), :], weight[b], ((1,), (1,)))

    def for_pair(i, carry):
        t = lax.rem(z + 1 + i, nz)
        pair_send[t] = part_of(2 * t + 1 - k).astype(jnp.bfloat16)
        pair_copy(t).start()
        return carry

    lax.fori_loop(0, nz, for_pair, 0)
    stage_b(0)
    gat_copy(r, None, 0, to_x).start()
    gat_copy(r, None, 1, to_y).start()
    stage_a(1)
    over_plane(1)

    def for_self(i, carry):
        t = lax.rem(z + 1 + i, nz)
        own[t] = part_of(2 * t + k)
        return carry

    lax.fori_loop(0, nz, for_self, 0)

    for t in range(nz):
        pair_copy(t).wait_recv()

    def line_copy(t, down, device):
        slot = t + nz if down else t
        return remote(
            line_send.at[t], line_recv.at[slot], ls_sent.at[t], lr_recv.at[slot], device
        )

    def hop(p, t):
        down = t < p
        summed = own[t] + pair_recv[t].astype(jnp.float32)
        if 0 < p < nz - 1:
            line_copy(t, down, pair).wait_recv()
            summed = summed + line_recv[t + nz if down else t].astype(jnp.float32)
        line_send[t] = summed.astype(jnp.bfloat16)
        to = col - 2 if down else col + 2
        line_copy(t, down, {"col": lax.rem(to + 2 * nz, 2 * nz)}).start()

    def line_step(tau):
        for p in range(nz):
            turns = []
            for t in range(nz):
                if t == p:
                    continue
                near, far = (p, t) if t > p else (nz - 1 - p, nz - 1 - t)
                turn = 0 if near == 0 else nz - 1 - far + near
                if turn == tau:
                    turns.append((-far, t))
            if turns:

                @pl.when(z == p)
                def _():
                    for _, t in sorted(turns):
                        hop(p, t)

    stage_a(2)
    stage_c(0)
    line_step(0)
    stage_m(0)
    stage_a(3)
    stage_c(1)
    gat_copy(xn, None, 0, to_x).wait_recv()
    gat_copy(xn, 0, 2, to_y).start()
    gat_copy(yn, None, 0, to_x).wait_recv()
    gat_copy(yn, 1, 3, to_x).start()
    over_plane(2)
    over_plane(3)
    line_step(1)
    stage_m(1)
    line_step(2)
    stage_b(1)
    stage_c(2)
    stage_m(2)
    stage_m(3)
    mixed_out[...] = (gate[...] * (total_acc[0] + total_acc[1])).astype(jnp.bfloat16)

    inner_chip = (z > 0) & (z < nz - 1)

    @pl.when(inner_chip)
    def _():
        stage_c(3)

    own[z] = own[z] + pair_recv[z].astype(jnp.float32)

    @pl.when(z > 0)
    def _():
        line_copy(z, False, pair).wait_recv()
        own[z] = own[z] + line_recv[z].astype(jnp.float32)

    @pl.when(z < nz - 1)
    def _():
        line_copy(z, True, pair).wait_recv()
        own[z] = own[z] + line_recv[nz + z].astype(jnp.float32)

    upstream[...] = own[z].astype(jnp.bfloat16)
    for h in range(heads):
        lanes = slice(h * HEAD, (h + 1) * HEAD)
        upper = upstream[:, lanes]
        probs = probs_s[h]
        grad_out[2, :, lanes] = dot(probs.astype(jnp.bfloat16), upper, ((0,), (0,))).astype(
            jnp.bfloat16
        )
        grad_probs = dot(upper, qkv[2, :, lanes], ((1,), (1,)))
        inner = jnp.sum(probs * grad_probs, axis=-1, keepdims=True)
        grad_scores = (probs * (grad_probs - inner)).astype(jnp.bfloat16)
        grad_out[0, :, lanes] = (
            dot(grad_scores, qkv[1, :, lanes], ((1,), (0,))) * factor
        ).astype(jnp.bfloat16)
        grad_out[1, :, lanes] = (
            dot(grad_scores, qkv[0, :, lanes], ((0,), (0,))) * factor
        ).astype(jnp.bfloat16)

    gat_copy(dn, 0, 0, to_x).wait_recv()
    gat_copy(dn, 1, 0, to_x).wait_recv()
    gat_out.start()
    stage_w(0)
    stage_b(2)
    stage_w(1)

    @pl.when(jnp.logical_not(inner_chip))
    def _():
        stage_c(3)

    stage_b(3)
    stage_w(2)
    stage_w(3)

    gat_copy(r, None, 0, to_x).wait_send()
    gat_copy(r, None, 1, to_y).wait_send()
    gat_copy(xn, 0, 2, to_y).wait_send()
    gat_copy(yn, 1, 3, to_x).wait_send()
    for j in range(nz):
        o = origins[j]
        b = 2 * o + k

        @pl.when((o <= z) & (z < nz - 1))
        def _():
            upward(0, o).wait_send()
            upward(1, o).wait_send()

        @pl.when((o >= z) & (z > 0))
        def _():
            downward(0, o).wait_send()
            downward(1, o).wait_send()

        att_copy(r, b, None, x_sent.at[j], to_x).wait_send()
        att_copy(r, b, None, y_sent.at[j], to_y).wait_send()
        if j == 0:
            att_copy(xn, b, 0, fy_sent.at[j], to_y).wait_send()
            att_copy(yn, b, 1, fx_sent.at[j], to_x).wait_send()
        for row in (r, xn, yn, dn):
            pass_on(row, o).wait_send()
        pair_copy(j).wait_send()
        for c in range(2):
            (out_copy if j < early else tail_copy)(j, c).wait()
    for d in range(1, nz):
        line_copy(lax.rem(z + d, nz), False, pair).wait_send()
    gat_out.wait()


def fused_device(
    qkv,
    out_weight,
    cotangent,
    scene_lengths,
    bucket_ids,
    sensor_ids,
    gsd_ids,
    step_ids,
    step_table,
    gsd_table,
    sensor_table,
    bucket_table,
):
    rows = lax.axis_size("row")
    cols = lax.axis_size("col")
    nz = cols // 2
    tok, width = cotangent.shape
    local = qkv.shape[2]
    early = nz - 1
    late = nz - early
    dma = pltpu.SemaphoreType.DMA
    bf16 = jnp.bfloat16
    mixed, grad, head, tail, gat_all = pl.pallas_call(
        fused_kernel,
        out_shape=(
            jax.ShapeDtypeStruct((tok, width), bf16),
            jax.ShapeDtypeStruct((3, tok, local), bf16),
            jax.ShapeDtypeStruct((early, 2, local, width), bf16),
            jax.ShapeDtypeStruct((late, 2, rows * tok, local), bf16),
            jax.ShapeDtypeStruct((rows * tok, width), bf16),
        ),
        in_specs=[pl.BlockSpec(memory_space=pltpu.SMEM)] * 5
        + [
            pl.BlockSpec(memory_space=pltpu.VMEM),
            pl.BlockSpec(memory_space=pl.ANY),
            pl.BlockSpec(memory_space=pltpu.VMEM),
            pl.BlockSpec(memory_space=pl.ANY),
        ]
        + [pl.BlockSpec(memory_space=pltpu.VMEM)] * 3,
        out_specs=(pl.BlockSpec(memory_space=pltpu.VMEM),) * 2
        + (pl.BlockSpec(memory_space=pl.ANY),) * 3,
        scratch_shapes=[
            pltpu.VMEM(step_table.shape, bf16),
            pltpu.VMEM((cols, local, width), bf16),
            pltpu.VMEM((cols, rows * tok, local), bf16),
            pltpu.VMEM((rows * tok, width), bf16),
            pltpu.VMEM((tok, width), jnp.float32),
            pltpu.VMEM((2, tok, width), jnp.float32),
            pltpu.VMEM((local // HEAD, tok, tok), jnp.float32),
            pltpu.VMEM((nz, tok, local), jnp.float32),
            pltpu.VMEM((nz, tok, local), bf16),
            pltpu.VMEM((nz, tok, local), bf16),
            pltpu.VMEM((nz, tok, local), bf16),
            pltpu.VMEM((2 * nz, tok, local), bf16),
            pltpu.VMEM((tok, local), bf16),
            dma((cols,)),
            dma,
            dma((early, 2)),
            dma((late, 2)),
            dma,
            dma((rows, cols, 2)),
            dma((rows, 2)),
            dma((nz,)),
            dma((2 * nz,)),
            dma((2, nz, 2)),
            dma((nz,)),
            dma((nz,)),
            dma((nz,)),
            dma((nz,)),
            dma((rows, nz)),
            dma((4,)),
            dma((nz,)),
            dma((nz,)),
        ],
        compiler_params=pltpu.CompilerParams(
            collective_id=0, has_side_effects=True, vmem_limit_bytes=60 * 2**20
        ),
        cost_estimate=pl.CostEstimate(
            flops=2 * (rows + 2) * tok * out_weight.shape[0] * width,
            bytes_accessed=4 * out_weight.shape[0] * width,
            transcendentals=0,
        ),
    )(
        scene_lengths,
        bucket_ids,
        sensor_ids,
        gsd_ids,
        step_ids,
        jnp.transpose(qkv, (1, 0, 2)),
        out_weight,
        cotangent,
        step_table,
        gsd_table,
        sensor_table,
        bucket_table,
    )
    mixed, grad, total = pl.pallas_call(
        last_kernel,
        out_shape=(
            jax.ShapeDtypeStruct(mixed.shape, bf16),
            jax.ShapeDtypeStruct(grad.shape, bf16),
            jax.ShapeDtypeStruct(out_weight.shape, bf16),
        ),
        in_specs=[pl.BlockSpec(memory_space=pl.ANY)] * 5,
        out_specs=(pl.BlockSpec(memory_space=pl.ANY),) * 3,
        scratch_shapes=[
            pltpu.VMEM(mixed.shape, bf16),
            pltpu.VMEM(grad.shape, bf16),
            pltpu.VMEM(head.shape, bf16),
            pltpu.VMEM(tail.shape, bf16),
            pltpu.VMEM(gat_all.shape, bf16),
            pltpu.VMEM((late, 2, local, width), bf16),
            dma((3,)),
            dma((early, 2)),
            dma((late, 2)),
            dma((2,)),
            dma((nz, 2)),
        ],
        compiler_params=pltpu.CompilerParams(vmem_limit_bytes=60 * 2**20),
        cost_estimate=pl.CostEstimate(
            flops=2 * rows * tok * late * 2 * local * width,
            bytes_accessed=6 * out_weight.shape[0] * width,
            transcendentals=0,
        ),
    )(mixed, grad, head, tail, gat_all)
    return (mixed, jnp.transpose(grad, (1, 0, 2)), total)


def solution(mesh):
    planes = mesh.shape["row"] == 4 and mesh.shape["col"] == 8
    return jax.shard_map(
        fused_device if planes else on_device,
        mesh=mesh,
        in_specs=(
            P("row", None, "col"),
            P(None, "col"),
            P("row", "col"),
            P("row"),
            P("row"),
            P("row"),
            P("row"),
            P("row"),
            P(None, "col"),
            P(None, "col"),
            P(None, "col"),
            P(None, "col"),
        ),
        out_specs=(P("row", "col"), P("row", None, "col"), P(None, "col")),
        check_vma=False,
    )
```

```python
import jax
import jax.numpy as jnp
from jax import lax
from jax.experimental import pallas as pl
from jax.experimental.pallas import tpu as pltpu
from jax.sharding import PartitionSpec as P

HEAD = 128


def scene_of(lengths, count):
    ends = jnp.cumsum(lengths)
    places = jnp.arange(count)
    return jnp.sum((places[:, None] >= ends[None, :]).astype(jnp.int32), axis=1)


def lookup(ids, table):
    picks = (ids[:, None] == jnp.arange(table.shape[0])[None, :]).astype(table.dtype)
    return jnp.dot(picks, table, preferred_element_type=jnp.float32)


def attend(queries, keys, values, same):
    factor = HEAD ** (-0.5)
    scores = jnp.einsum("the,she->hts", queries, keys, preferred_element_type=jnp.float32) * factor
    scores = jnp.where(same[None], scores, -1e30)
    top = jnp.max(scores, axis=-1, keepdims=True)
    weights = jnp.exp(scores - top)
    probs = weights / jnp.sum(weights, axis=-1, keepdims=True)
    rounded = probs.astype(jnp.bfloat16)
    output = jnp.einsum("hts,she->the", rounded, values, preferred_element_type=jnp.float32).astype(
        jnp.bfloat16
    )
    return (probs, rounded, output)


def attend_back(queries, keys, values, probs, rounded, upstream):
    factor = HEAD ** (-0.5)
    grad_values = jnp.einsum(
        "hts,the->she", rounded, upstream, preferred_element_type=jnp.float32
    ).astype(jnp.bfloat16)
    grad_probs = jnp.einsum("the,she->hts", upstream, values, preferred_element_type=jnp.float32)
    inner = jnp.sum(probs * grad_probs, axis=-1, keepdims=True)
    grad_scores = (probs * (grad_probs - inner)).astype(jnp.bfloat16)
    grad_queries = (
        jnp.einsum("hts,she->the", grad_scores, keys, preferred_element_type=jnp.float32) * factor
    ).astype(jnp.bfloat16)
    grad_keys = (
        jnp.einsum("hts,the->she", grad_scores, queries, preferred_element_type=jnp.float32)
        * factor
    ).astype(jnp.bfloat16)
    stacked = jnp.stack([grad_queries, grad_keys, grad_values], axis=1)
    return stacked.reshape(stacked.shape[0], 3, stacked.shape[2] * stacked.shape[3])


def on_device(
    qkv,
    out_weight,
    cotangent,
    scene_lengths,
    bucket_ids,
    sensor_ids,
    gsd_ids,
    step_ids,
    step_table,
    gsd_table,
    sensor_table,
    bucket_table,
):
    tok_rows = qkv.shape[0]
    local_width = qkv.shape[2]
    heads_here = local_width // HEAD
    gate_scene = lookup(step_ids, step_table) + lookup(gsd_ids, gsd_table)
    gate_scene = gate_scene + lookup(sensor_ids, sensor_table) + lookup(bucket_ids, bucket_table)
    segments = scene_of(scene_lengths, tok_rows)
    member = (segments[:, None] == jnp.arange(scene_lengths.shape[0])[None, :]).astype(jnp.float32)
    gate = jnp.dot(
        member, gate_scene, precision=lax.Precision.HIGHEST, preferred_element_type=jnp.float32
    )
    same = segments[:, None] == segments[None, :]
    block = qkv.reshape(tok_rows, 3, heads_here, HEAD)
    queries = block[:, 0]
    keys = block[:, 1]
    values = block[:, 2]
    probs, rounded, attended = attend(queries, keys, values, same)
    attended = attended.reshape(tok_rows, local_width)
    rows = out_weight
    projected = jnp.dot(
        lax.all_gather(attended, "col", axis=1, tiled=True),
        rows,
        preferred_element_type=jnp.float32,
    )
    mixed = (gate * projected).astype(jnp.bfloat16)
    gated = (gate * cotangent.astype(jnp.float32)).astype(jnp.bfloat16)
    rows = out_weight
    summed = lax.psum_scatter(
        lax.dot_general(
            rows, gated, (((1,), (1,)), ((), ())), preferred_element_type=jnp.float32
        ).astype(jnp.bfloat16),
        "col",
        scatter_dimension=0,
        tiled=True,
    )
    upstream = summed.T.reshape(tok_rows, heads_here, HEAD)
    grad_qkv = attend_back(queries, keys, values, probs, rounded, upstream)
    partial_sum = lax.dot_general(
        lax.all_gather(attended, "col", axis=1, tiled=True),
        gated,
        (((0,), (0,)), ((), ())),
        preferred_element_type=jnp.float32,
    )
    total = lax.psum(partial_sum.astype(jnp.bfloat16), "row")
    return (mixed, grad_qkv, total)


def dot(a, b, dims):
    return lax.dot_general(a, b, (dims, ((), ())), preferred_element_type=jnp.float32)


def remote(src, dst, send, recv, device):
    return pltpu.make_async_remote_copy(
        src_ref=src,
        dst_ref=dst,
        send_sem=send,
        recv_sem=recv,
        device_id=device,
        device_id_type=pl.DeviceIdType.MESH,
    )


def origins_of(z, nz):
    orders = [
        sorted(range(nz), key=lambda o: (abs(o - p), -o if 2 * p < nz else o)) for p in range(nz)
    ]
    origins = []
    for j in range(nz):
        picked = orders[0][j]
        for p in range(1, nz):
            picked = jnp.where(z == p, orders[p][j], picked)
        origins.append(picked)
    return origins


def last_kernel(
    mixed_in,
    grad_in,
    total_head,
    att_tail,
    gat_all,
    mixed_out,
    grad_out,
    total_out,
    mixed,
    grad,
    head,
    att,
    gat,
    tail,
    in_sem,
    head_sem,
    att_sem,
    out_sem,
    total_sem,
):
    early, parts, local, width = head.shape
    late = att.shape[0]
    origins = origins_of(lax.axis_index("col") // 2, early + late)

    def place(j, c):
        return total_out.at[pl.ds(pl.multiple_of((2 * origins[j] + c) * local, local), local)]

    gat_load = pltpu.make_async_copy(gat_all, gat, in_sem.at[0])
    gat_load.start()
    att_loads = {}
    for j in range(late):
        for c in range(parts):
            att_loads[j, c] = pltpu.make_async_copy(att_tail.at[j, c], att.at[j, c], att_sem.at[j, c])
            att_loads[j, c].start()
    moves = []
    for j in range(early):
        for c in range(parts):
            moves.append((
                pltpu.make_async_copy(total_head.at[j, c], head.at[j, c], head_sem.at[j, c]),
                pltpu.make_async_copy(head.at[j, c], place(j, c), total_sem.at[j, c]),
            ))
    moves.append((
        pltpu.make_async_copy(mixed_in, mixed, in_sem.at[1]),
        pltpu.make_async_copy(mixed, mixed_out, out_sem.at[0]),
    ))
    moves.append((
        pltpu.make_async_copy(grad_in, grad, in_sem.at[2]),
        pltpu.make_async_copy(grad, grad_out, out_sem.at[1]),
    ))
    for load, store in moves:
        load.start()
    gat_load.wait()
    steps = late * parts
    share = -(-len(moves) // steps)
    stores = []
    for i in range(steps):
        j, c = divmod(i, parts)
        att_loads[j, c].wait()
        tail[j, c] = dot(att[j, c], gat[...], ((0,), (0,))).astype(jnp.bfloat16)
        stores.append(pltpu.make_async_copy(tail.at[j, c], place(early + j, c), total_sem.at[early + j, c]))
        stores[-1].start()
        for load, store in moves[i * share : (i + 1) * share]:
            load.wait()
            store.start()
            stores.append(store)
    for store in stores:
        store.wait()


def fused_kernel(
    lengths,
    bucket_ids,
    sensor_ids,
    gsd_ids,
    step_ids,
    qkv,
    weight_hbm,
    cotangent,
    step_hbm,
    gsd_table,
    sensor_table,
    bucket_table,
    mixed_out,
    grad_out,
    total_head,
    att_tail,
    gat_all,
    step_table,
    weight,
    att,
    gat,
    gate,
    total_acc,
    probs_s,
    own,
    pair_send,
    pair_recv,
    line_send,
    line_recv,
    upstream,
    w_sem,
    step_sem,
    out_sem,
    tail_sem,
    gat_sem,
    att_recv,
    gat_recv,
    pr_recv,
    lr_recv,
    z_sent,
    x_sent,
    y_sent,
    fx_sent,
    fy_sent,
    p_sent,
    g_sent,
    ps_sent,
    ls_sent,
):
    tok, width = cotangent.shape
    local = qkv.shape[2]
    heads = local // HEAD
    half = tok // 2
    nb = weight.shape[0]
    nz = nb // 2
    scenes = lengths.shape[0]
    early = total_head.shape[0]
    factor = HEAD ** (-0.5)
    r = lax.axis_index("row")
    col = lax.axis_index("col")
    z = col // 2
    k = lax.rem(col, 2)
    xn = r + 1 - 2 * lax.rem(r, 2)
    yn = lax.rem(r + 2, 4)
    dn = 3 - r
    pair = {"col": col + 1 - 2 * k}
    to_x = {"row": xn}
    to_y = {"row": yn}

    barrier = pltpu.get_barrier_semaphore()
    peers = [pair, to_x, to_y] + [{"col": 2 * lax.rem(z + d, nz) + k} for d in range(1, nz)]
    for peer in peers:
        pl.semaphore_signal(
            barrier, inc=1, device_id=peer, device_id_type=pl.DeviceIdType.MESH
        )
    pl.semaphore_wait(barrier, len(peers))

    def load(b):
        return pltpu.make_async_copy(
            weight_hbm.at[pl.ds(b * local, local)], weight.at[b], w_sem.at[b]
        )

    step_load = pltpu.make_async_copy(step_hbm, step_table, step_sem)
    step_load.start()
    for b in range(nb):
        load(b).start()

    def token_rows(row, part=None):
        if part is None:
            return pl.ds(pl.multiple_of(row * tok, tok), tok)
        return pl.ds(pl.multiple_of(row * tok + part * half, half), half)

    place_col = lax.broadcasted_iota(jnp.int32, (tok, 1), 0)
    place_row = lax.broadcasted_iota(jnp.int32, (1, tok), 1)
    seg_col = jnp.zeros((tok, 1), jnp.int32)
    seg_row = jnp.zeros((1, tok), jnp.int32)
    end = 0
    for s in range(scenes):
        end = end + lengths[s]
        seg_col = seg_col + (place_col >= end).astype(jnp.int32)
        seg_row = seg_row + (place_row >= end).astype(jnp.int32)

    same = seg_col == seg_row
    mine = 2 * z + k
    for h in range(heads):
        lanes = slice(h * HEAD, (h + 1) * HEAD)
        scores = dot(qkv[0, :, lanes], qkv[1, :, lanes], ((1,), (1,))) * factor
        scores = jnp.where(same, scores, -1e30)
        top = jnp.max(scores, axis=-1, keepdims=True)
        weights = jnp.exp(scores - top)
        probs = weights / jnp.sum(weights, axis=-1, keepdims=True)
        probs_s[h] = probs
        out = dot(probs.astype(jnp.bfloat16), qkv[2, :, lanes], ((1,), (0,)))
        att[mine, token_rows(r), lanes] = out.astype(jnp.bfloat16)

    origins = origins_of(z, nz)

    def block(row, b, part=None):
        return att.at[b, token_rows(row, part)]

    def att_copy(row, b, part, send, device):
        ref = block(row, b, part)
        return remote(ref, ref, send, att_recv.at[row, b, 0 if part is None else part], device)

    def pass_on(row, o):
        return att_copy(row, 2 * o + k, None, p_sent.at[row, o], pair)

    def got(row, b, part=None):
        att_copy(row, b, part, p_sent.at[0, 0], pair).wait_recv()

    def upward(which, o):
        row = dn if which else r
        return att_copy(
            row, 2 * o + k, None, z_sent.at[which, o, 0], {"col": lax.rem(col + 2, 2 * nz)}
        )

    def downward(which, o):
        row = dn if which else r
        return att_copy(
            row, 2 * o + k, None, z_sent.at[which, o, 1], {"col": lax.rem(col + 2 * nz - 2, 2 * nz)}
        )

    def along_z(which, o):
        @pl.when((o <= z) & (z < nz - 1))
        def _():
            upward(which, o).start()

        @pl.when((o >= z) & (z > 0))
        def _():
            downward(which, o).start()

    def stage_a(j):
        o = origins[j]
        if j > 0:
            got(r, 2 * o + k)
        along_z(0, o)
        pass_on(r, o).start()

    def over_plane(j):
        o = origins[j]
        att_copy(r, 2 * o + k, None, x_sent.at[j], to_x).start()
        att_copy(r, 2 * o + k, None, y_sent.at[j], to_y).start()

    def stage_b(j):
        o = origins[j]
        b = 2 * o + k
        got(xn, b)
        if j == 0:
            att_copy(xn, b, 0, fy_sent.at[j], to_y).start()
        pass_on(xn, o).start()
        got(yn, b)
        if j == 0:
            att_copy(yn, b, 1, fx_sent.at[j], to_x).start()
        pass_on(yn, o).start()

    def stage_c(j):
        o = origins[j]
        if j == 0:
            got(dn, 2 * o + k, 0)
            got(dn, 2 * o + k, 1)
        else:
            got(dn, 2 * o + k)
        along_z(1, o)
        pass_on(dn, o).start()

    def stage_m(j):
        o = origins[j]
        got(r, 2 * o + 1 - k)

        def add(c, carry):
            b = 2 * o + c
            term = dot(att[b, token_rows(r), :], weight[b], ((1,), (0,)))
            if j == 0:
                total_acc[c] = term
            else:
                total_acc[c] += term
            return carry

        lax.fori_loop(0, 2, add, 0)

    def out_copy(j, c):
        return pltpu.make_async_copy(
            weight.at[2 * origins[j] + c], total_head.at[j, c], out_sem.at[j, c]
        )

    def tail_copy(j, c):
        return pltpu.make_async_copy(
            att.at[2 * origins[j] + c], att_tail.at[j - early, c], tail_sem.at[j - early, c]
        )

    gat_out = pltpu.make_async_copy(gat, gat_all, gat_sem)

    def stage_w(j):
        o = origins[j]
        for row in (xn, yn, dn):
            got(row, 2 * o + 1 - k)

        def form(c, carry):
            b = 2 * o + c
            weight[b] = dot(att[b], gat[...], ((0,), (0,))).astype(jnp.bfloat16)
            out_copy(j, c).start()
            return carry

        if j < early:
            lax.fori_loop(0, 2, form, 0)
        else:
            for c in range(2):
                tail_copy(j, c).start()

    over_plane(0)
    stage_a(0)

    def picks(ids, table):
        count = table.shape[0]
        which = lax.broadcasted_iota(jnp.int32, (scenes, count), 0)
        place = lax.broadcasted_iota(jnp.int32, (scenes, count), 1)
        wanted = jnp.zeros((scenes, count), jnp.int32)
        for s in range(scenes):
            wanted = jnp.where(which == s, ids[s], wanted)
        chosen = jnp.where(place == wanted, 1.0, 0.0).astype(table.dtype)
        return dot(chosen, table[...], ((1,), (0,)))

    step_load.wait()
    gate_scene = picks(step_ids, step_table) + picks(gsd_ids, gsd_table)
    gate_scene = gate_scene + picks(sensor_ids, sensor_table) + picks(bucket_ids, bucket_table)
    value = jnp.broadcast_to(gate_scene[0:1, :], (tok, width))
    for s in range(1, scenes):
        value = jnp.where(seg_col == s, gate_scene[s : s + 1, :], value)
    gate[...] = value
    gat[token_rows(r), :] = (value * cotangent[...].astype(jnp.float32)).astype(jnp.bfloat16)

    def gat_copy(row, part, send, device):
        rows = gat.at[token_rows(row, part)]
        return remote(rows, rows, g_sent.at[send], gat_recv.at[row, 0 if part is None else part], device)


    for b in range(nb):
        load(b).wait()

    def pair_copy(t):
        return remote(pair_send.at[t], pair_recv.at[t], ps_sent.at[t], pr_recv.at[t], pair)

    def part_of(b):
        return dot(gat[token_rows(r), :], weight[b], ((1,), (1,)))

    def for_pair(i, carry):
        t = lax.rem(z + 1 + i, nz)
        pair_send[t] = part_of(2 * t + 1 - k).astype(jnp.bfloat16)
        pair_copy(t).start()
        return carry

    lax.fori_loop(0, nz, for_pair, 0)
    stage_b(0)
    gat_copy(r, None, 0, to_x).start()
    gat_copy(r, None, 1, to_y).start()
    stage_a(1)
    over_plane(1)

    def for_self(i, carry):
        t = lax.rem(z + 1 + i, nz)
        own[t] = part_of(2 * t + k)
        return carry

    lax.fori_loop(0, nz, for_self, 0)

    for t in range(nz):
        pair_copy(t).wait_recv()

    def line_copy(t, down, device):
        slot = t + nz if down else t
        return remote(
            line_send.at[t], line_recv.at[slot], ls_sent.at[t], lr_recv.at[slot], device
        )

    def hop(p, t):
        down = t < p
        summed = own[t] + pair_recv[t].astype(jnp.float32)
        if 0 < p < nz - 1:
            line_copy(t, down, pair).wait_recv()
            summed = summed + line_recv[t + nz if down else t].astype(jnp.float32)
        line_send[t] = summed.astype(jnp.bfloat16)
        to = col - 2 if down else col + 2
        line_copy(t, down, {"col": lax.rem(to + 2 * nz, 2 * nz)}).start()

    def line_step(tau):
        for p in range(nz):
            turns = []
            for t in range(nz):
                if t == p:
                    continue
                near, far = (p, t) if t > p else (nz - 1 - p, nz - 1 - t)
                turn = 0 if near == 0 else nz - 1 - far + near
                if turn == tau:
                    turns.append((-far, t))
            if turns:

                @pl.when(z == p)
                def _():
                    for _, t in sorted(turns):
                        hop(p, t)

    stage_a(2)
    stage_c(0)
    line_step(0)
    stage_m(0)
    stage_a(3)
    stage_c(1)
    gat_copy(xn, None, 0, to_x).wait_recv()
    gat_copy(xn, 0, 2, to_y).start()
    gat_copy(yn, None, 0, to_x).wait_recv()
    gat_copy(yn, 1, 3, to_x).start()
    over_plane(2)
    over_plane(3)
    line_step(1)
    stage_m(1)
    line_step(2)
    stage_b(1)
    stage_c(2)
    stage_m(2)
    stage_m(3)
    mixed_out[...] = (gate[...] * (total_acc[0] + total_acc[1])).astype(jnp.bfloat16)

    inner_chip = (z > 0) & (z < nz - 1)

    @pl.when(inner_chip)
    def _():
        stage_c(3)

    own[z] = own[z] + pair_recv[z].astype(jnp.float32)

    @pl.when(z > 0)
    def _():
        line_copy(z, False, pair).wait_recv()
        own[z] = own[z] + line_recv[z].astype(jnp.float32)

    @pl.when(z < nz - 1)
    def _():
        line_copy(z, True, pair).wait_recv()
        own[z] = own[z] + line_recv[nz + z].astype(jnp.float32)

    upstream[...] = own[z].astype(jnp.bfloat16)
    for h in range(heads):
        lanes = slice(h * HEAD, (h + 1) * HEAD)
        upper = upstream[:, lanes]
        probs = probs_s[h]
        grad_out[2, :, lanes] = dot(probs.astype(jnp.bfloat16), upper, ((0,), (0,))).astype(
            jnp.bfloat16
        )
        grad_probs = dot(upper, qkv[2, :, lanes], ((1,), (1,)))
        inner = jnp.sum(probs * grad_probs, axis=-1, keepdims=True)
        grad_scores = (probs * (grad_probs - inner)).astype(jnp.bfloat16)
        grad_out[0, :, lanes] = (
            dot(grad_scores, qkv[1, :, lanes], ((1,), (0,))) * factor
        ).astype(jnp.bfloat16)
        grad_out[1, :, lanes] = (
            dot(grad_scores, qkv[0, :, lanes], ((0,), (0,))) * factor
        ).astype(jnp.bfloat16)

    gat_copy(dn, 0, 0, to_x).wait_recv()
    gat_copy(dn, 1, 0, to_x).wait_recv()
    gat_out.start()
    stage_w(0)
    stage_b(2)
    stage_w(1)

    @pl.when(jnp.logical_not(inner_chip))
    def _():
        stage_c(3)

    stage_b(3)
    stage_w(2)
    stage_w(3)

    gat_copy(r, None, 0, to_x).wait_send()
    gat_copy(r, None, 1, to_y).wait_send()
    gat_copy(xn, 0, 2, to_y).wait_send()
    gat_copy(yn, 1, 3, to_x).wait_send()
    for j in range(nz):
        o = origins[j]
        b = 2 * o + k

        @pl.when((o <= z) & (z < nz - 1))
        def _():
            upward(0, o).wait_send()
            upward(1, o).wait_send()

        @pl.when((o >= z) & (z > 0))
        def _():
            downward(0, o).wait_send()
            downward(1, o).wait_send()

        att_copy(r, b, None, x_sent.at[j], to_x).wait_send()
        att_copy(r, b, None, y_sent.at[j], to_y).wait_send()
        if j == 0:
            att_copy(xn, b, 0, fy_sent.at[j], to_y).wait_send()
            att_copy(yn, b, 1, fx_sent.at[j], to_x).wait_send()
        for row in (r, xn, yn, dn):
            pass_on(row, o).wait_send()
        pair_copy(j).wait_send()
        for c in range(2):
            (out_copy if j < early else tail_copy)(j, c).wait()
    for d in range(1, nz):
        line_copy(lax.rem(z + d, nz), False, pair).wait_send()
    gat_out.wait()


def fused_device(
    qkv,
    out_weight,
    cotangent,
    scene_lengths,
    bucket_ids,
    sensor_ids,
    gsd_ids,
    step_ids,
    step_table,
    gsd_table,
    sensor_table,
    bucket_table,
):
    rows = lax.axis_size("row")
    cols = lax.axis_size("col")
    nz = cols // 2
    tok, width = cotangent.shape
    local = qkv.shape[2]
    early = nz - 2
    late = nz - early
    dma = pltpu.SemaphoreType.DMA
    bf16 = jnp.bfloat16
    mixed, grad, head, tail, gat_all = pl.pallas_call(
        fused_kernel,
        out_shape=(
            jax.ShapeDtypeStruct((tok, width), bf16),
            jax.ShapeDtypeStruct((3, tok, local), bf16),
            jax.ShapeDtypeStruct((early, 2, local, width), bf16),
            jax.ShapeDtypeStruct((late, 2, rows * tok, local), bf16),
            jax.ShapeDtypeStruct((rows * tok, width), bf16),
        ),
        in_specs=[pl.BlockSpec(memory_space=pltpu.SMEM)] * 5
        + [
            pl.BlockSpec(memory_space=pltpu.VMEM),
            pl.BlockSpec(memory_space=pl.ANY),
            pl.BlockSpec(memory_space=pltpu.VMEM),
            pl.BlockSpec(memory_space=pl.ANY),
        ]
        + [pl.BlockSpec(memory_space=pltpu.VMEM)] * 3,
        out_specs=(pl.BlockSpec(memory_space=pltpu.VMEM),) * 2
        + (pl.BlockSpec(memory_space=pl.ANY),) * 3,
        scratch_shapes=[
            pltpu.VMEM(step_table.shape, bf16),
            pltpu.VMEM((cols, local, width), bf16),
            pltpu.VMEM((cols, rows * tok, local), bf16),
            pltpu.VMEM((rows * tok, width), bf16),
            pltpu.VMEM((tok, width), jnp.float32),
            pltpu.VMEM((2, tok, width), jnp.float32),
            pltpu.VMEM((local // HEAD, tok, tok), jnp.float32),
            pltpu.VMEM((nz, tok, local), jnp.float32),
            pltpu.VMEM((nz, tok, local), bf16),
            pltpu.VMEM((nz, tok, local), bf16),
            pltpu.VMEM((nz, tok, local), bf16),
            pltpu.VMEM((2 * nz, tok, local), bf16),
            pltpu.VMEM((tok, local), bf16),
            dma((cols,)),
            dma,
            dma((early, 2)),
            dma((late, 2)),
            dma,
            dma((rows, cols, 2)),
            dma((rows, 2)),
            dma((nz,)),
            dma((2 * nz,)),
            dma((2, nz, 2)),
            dma((nz,)),
            dma((nz,)),
            dma((nz,)),
            dma((nz,)),
            dma((rows, nz)),
            dma((4,)),
            dma((nz,)),
            dma((nz,)),
        ],
        compiler_params=pltpu.CompilerParams(
            collective_id=0, has_side_effects=True, vmem_limit_bytes=60 * 2**20
        ),
        cost_estimate=pl.CostEstimate(
            flops=2 * (rows + 2) * tok * out_weight.shape[0] * width,
            bytes_accessed=4 * out_weight.shape[0] * width,
            transcendentals=0,
        ),
    )(
        scene_lengths,
        bucket_ids,
        sensor_ids,
        gsd_ids,
        step_ids,
        jnp.transpose(qkv, (1, 0, 2)),
        out_weight,
        cotangent,
        step_table,
        gsd_table,
        sensor_table,
        bucket_table,
    )
    mixed, grad, total = pl.pallas_call(
        last_kernel,
        out_shape=(
            jax.ShapeDtypeStruct(mixed.shape, bf16),
            jax.ShapeDtypeStruct(grad.shape, bf16),
            jax.ShapeDtypeStruct(out_weight.shape, bf16),
        ),
        in_specs=[pl.BlockSpec(memory_space=pl.ANY)] * 5,
        out_specs=(pl.BlockSpec(memory_space=pl.ANY),) * 3,
        scratch_shapes=[
            pltpu.VMEM(mixed.shape, bf16),
            pltpu.VMEM(grad.shape, bf16),
            pltpu.VMEM(head.shape, bf16),
            pltpu.VMEM(tail.shape, bf16),
            pltpu.VMEM(gat_all.shape, bf16),
            pltpu.VMEM((late, 2, local, width), bf16),
            dma((3,)),
            dma((early, 2)),
            dma((late, 2)),
            dma((2,)),
            dma((nz, 2)),
        ],
        compiler_params=pltpu.CompilerParams(vmem_limit_bytes=60 * 2**20),
        cost_estimate=pl.CostEstimate(
            flops=2 * rows * tok * late * 2 * local * width,
            bytes_accessed=6 * out_weight.shape[0] * width,
            transcendentals=0,
        ),
    )(mixed, grad, head, tail, gat_all)
    return (mixed, jnp.transpose(grad, (1, 0, 2)), total)


def solution(mesh):
    planes = mesh.shape["row"] == 4 and mesh.shape["col"] == 8
    return jax.shard_map(
        fused_device if planes else on_device,
        mesh=mesh,
        in_specs=(
            P("row", None, "col"),
            P(None, "col"),
            P("row", "col"),
            P("row"),
            P("row"),
            P("row"),
            P("row"),
            P("row"),
            P(None, "col"),
            P(None, "col"),
            P(None, "col"),
            P(None, "col"),
        ),
        out_specs=(P("row", "col"), P("row", None, "col"), P(None, "col")),
        check_vma=False,
    )
```
